512 devices in a mesh: ctx: 16 (over z), head: 32 (over x, y, core).
Axes of the slice: x: 4, y: 4, z: 16, core: 2. Of those that a mesh axis runs over, the one named last changes fastest.
Arguments:
- mixer_input: bfloat16 [8192, 8192], P('ctx', 'head')
- gate_input: bfloat16 [8192, 8192], P('ctx', 'head'), may hold values from -6 to 6
- step_raw: float32 [8192, 128], P('ctx', 'head'), may hold values from -16 to 4
- decay_log: float32 [128], P('head'), may hold values from -1.39 to -0.28
- skip_weight: float32 [128], P('head'), may hold values from 0.5 to 1.5
- state_maps: bfloat16 [8192, 2, 8, 128], P('ctx'), may hold values from -6 to 6
- norm_gain: float32 [8192], P('head'), may hold values from 0.25 to 1.75
- queries: bfloat16 [8192, 8192], P('ctx', 'head')
- keys_values: bfloat16 [8192, 2, 8, 128], P('ctx')
Outputs:
- mamba_out: bfloat16 [8192, 8192], P('ctx', 'head')
- attn_out: bfloat16 [8192, 8192], P('ctx', 'head')
The draws below stay inside these ranges and needn't reach their ends.
All inputs are finite; a program needn't handle non-finite values.
Results may differ from the reference program's by a relative error of at most 0.017.
Values may be sent and summed in bfloat16 or wider, within the bound.
A program may use at most 64 MiB of HBM per device.

```python
import math
import jax
import jax.numpy as jnp
from jax import lax

MIXER_HEADS = 128
HEAD_P = 64
STATE = 128
GROUPS = 8
Q_HEADS = 64
KV_HEADS = 8
ATT_HD = 128
SPAN = 128
TOK_DEV = 512
SEQUENCE_LENGTH = 8192


def head_magnitude(key):
    return jax.random.uniform(jax.random.fold_in(key, 101), (MIXER_HEADS,), jnp.float32, 0.25, 0.75)


def attention_draws(key):
    key_keys, key_values, key_queries = jax.random.split(key, 3)
    key_part = jax.random.normal(key_keys, (SEQUENCE_LENGTH, KV_HEADS, ATT_HD), jnp.float32)
    value_part = jax.random.normal(key_values, (SEQUENCE_LENGTH, KV_HEADS, ATT_HD), jnp.float32)
    query_part = jax.random.normal(key_queries, (SEQUENCE_LENGTH, Q_HEADS, ATT_HD), jnp.float32)
    for anchor in range(8):
        root = anchor * (SEQUENCE_LENGTH // 8) + 1
        key_part = key_part.at[root + 1].set(key_part[root + 1])
        query_part = query_part.at[root + 3].set(query_part[root + 3])
    return (query_part, key_part, value_part)


def draw_mixer_input(key, part):
    key = jax.random.fold_in(key, 13)
    key_body, key_rows, key_heads = jax.random.split(key, 3)
    values = jax.random.normal(key_body, (SEQUENCE_LENGTH, MIXER_HEADS * HEAD_P), jnp.float32)
    head_scale = jnp.exp(jax.random.uniform(key_heads, (MIXER_HEADS,), jnp.float32, 0.0, math.log(10.0)))
    row_scale = jnp.exp(jax.random.uniform(key_rows, (SEQUENCE_LENGTH, 1), jnp.float32, 0.0, math.log(10.0)))
    return (values * row_scale * jnp.repeat(head_scale, HEAD_P)[None, :]).astype(jnp.bfloat16)


def draw_decay_log(key, part):
    spike_size = head_magnitude(key)
    return jnp.log(spike_size)


def draw_step_raw(key, part):
    spike_size = head_magnitude(key)
    key = jax.random.fold_in(key, 3)
    lasting_share = 0.5
    random_key_persistent, random_key_noise, random_key_shift, random_key_spike, random_key_dropout = jax.random.split(key, 5)
    lasting = jax.random.bernoulli(random_key_persistent, lasting_share, (MIXER_HEADS,))
    fast_rate = max(1.0 / 40.0, 2.0 / TOK_DEV)
    base_rate = jnp.where(lasting, 1.0 / SEQUENCE_LENGTH, fast_rate)
    jitter = jax.random.uniform(random_key_noise, (SEQUENCE_LENGTH, MIXER_HEADS), jnp.float32, -0.7, 0.7)
    offset = jax.random.uniform(random_key_shift, (SEQUENCE_LENGTH // TOK_DEV, MIXER_HEADS), jnp.float32, -0.35, 0.35)
    offset = jnp.repeat(offset, TOK_DEV, axis=0)
    delta_widths = base_rate[None, :] / spike_size[None, :] * jnp.exp(jitter + offset)
    position_slots = jax.random.randint(random_key_spike, (3, MIXER_HEADS), 0, SEQUENCE_LENGTH)
    spike_events = jnp.any(jnp.arange(SEQUENCE_LENGTH)[:, None, None] == position_slots[None, :, :], axis=1)
    spike_weight_loss = jax.random.uniform(random_key_dropout, (SEQUENCE_LENGTH, MIXER_HEADS), jnp.float32, 0.2, 0.4)
    delta_widths = jnp.where(spike_events, spike_weight_loss / spike_size[None, :], delta_widths)
    return jnp.log(jnp.expm1(delta_widths))


def draw_queries(key, part):
    query_part, key_part, value_part = attention_draws(key)
    return query_part.reshape(SEQUENCE_LENGTH, Q_HEADS * ATT_HD).astype(jnp.bfloat16)


def draw_keys_values(key, part):
    query_part, key_part, value_part = attention_draws(key)
    return jnp.stack([key_part, value_part], axis=1).astype(jnp.bfloat16)


def steps_of(stream_key, extent, pieces, low, top_value):
    level = 1.0
    for axis_at, blocks in pieces:
        steps = jax.random.uniform(jax.random.fold_in(jax.random.fold_in(stream_key, 6), axis_at), (blocks,), jnp.float32, low / len(pieces), top_value / len(pieces))
        level = level * jnp.repeat(jnp.exp(steps), extent[axis_at] // blocks).reshape((-1,) + (1,) * (len(extent) - 1 - axis_at))
    return level


def scatter_about(key, extent, scale, reach, shards=(), held_as=jnp.bfloat16):
    values = jax.random.normal(key, extent, jnp.float32) * scale
    if len(shards) > 0:
        values = steps_of(key, extent, shards, -0.22, 0.18) * values
    return jnp.clip(values, min=-reach, max=reach).astype(held_as)


def setup_inputs(seed: int = 0) -> dict:
    key_of = jax.random.split(jax.random.key(seed), 10)
    return {
        "mixer_input": draw_mixer_input(jax.random.fold_in(key_of[9], 71), 0),
        "gate_input": scatter_about(key_of[1], (SEQUENCE_LENGTH, MIXER_HEADS * HEAD_P), 1.0, 6.0, ((0, 16), (1, 32))),
        "step_raw": draw_step_raw(jax.random.fold_in(key_of[9], 71), 0),
        "decay_log": draw_decay_log(jax.random.fold_in(key_of[9], 71), 0),
        "skip_weight": jnp.clip(0.5 + 1.0 * jax.random.uniform(key_of[4], (MIXER_HEADS,), jnp.float32) ** steps_of(key_of[4], (MIXER_HEADS,), ((0, 32),), -0.2, 0.2), 0.5, 1.5),
        "state_maps": scatter_about(key_of[5], (SEQUENCE_LENGTH, 2, GROUPS, STATE), 1.0, 6.0, ((0, 16),)),
        "norm_gain": jnp.clip(1.0 + 0.15 * jax.random.normal(key_of[6], (MIXER_HEADS * HEAD_P,), jnp.float32), 0.25, 1.75),
        "queries": draw_queries(jax.random.fold_in(key_of[9], 71), 0),
        "keys_values": draw_keys_values(jax.random.fold_in(key_of[9], 71), 0),
    }


NEG_FILL = -1e+30
EPSILON = 1e-05

def span_pass(x_rows, dt_rows, decay_rate, b_rows, c_rows):
    length, head_count, head_width = x_rows.shape
    block_count = length // SPAN
    logs_rows = dt_rows * decay_rate[None, :]
    offsets = jnp.arange(SPAN)
    below_diag = offsets[:, None] >= offsets[None, :]

    def advance(running, inputs):
        x_block, dt_block, log_block, b_block, c_block = inputs
        cumulative = jnp.cumsum(log_block, axis=0)
        cumul_heads = cumulative.T
        spread = jnp.where(below_diag[None], cumul_heads[:, :, None] - cumul_heads[:, None, :], NEG_FILL)
        scores = jnp.dot(c_block, b_block.T, preferred_element_type=jnp.float32)
        weights = (scores[None] * jnp.exp(spread) * dt_block.T[:, None, :]).astype(jnp.bfloat16)
        inside = jnp.einsum('hts,shp->thp', weights.astype(jnp.float32), x_block.astype(jnp.float32))
        carried = jnp.einsum('tn,hnp->thp', c_block.astype(jnp.float32), running, precision=lax.Precision.HIGHEST)
        carried = carried * jnp.exp(cumulative)[:, :, None]
        tail_decay = jnp.exp(cumulative[-1][None, :] - cumulative) * dt_block
        state_loads = (tail_decay.T[:, :, None] * b_block.astype(jnp.float32)[None, :, :]).astype(jnp.bfloat16)
        fresh_state = jnp.einsum('hsn,shp->hnp', state_loads.astype(jnp.float32), x_block.astype(jnp.float32))
        running = jnp.exp(cumulative[-1])[:, None, None] * running + fresh_state
        return (running, inside + carried)
    blocks = (x_rows.reshape(block_count, SPAN, head_count, head_width), dt_rows.reshape(block_count, SPAN, head_count), logs_rows.reshape(block_count, SPAN, head_count), b_rows.reshape(block_count, SPAN, b_rows.shape[1]), c_rows.reshape(block_count, SPAN, c_rows.shape[1]))
    starting = jnp.zeros((head_count, b_rows.shape[1], head_width), jnp.float32)
    final_state, outputs = lax.scan(advance, starting, blocks)
    return (outputs.reshape(length, head_count, head_width), final_state)

def reference(mixer_input, gate_input, step_raw, decay_log, skip_weight, state_maps, norm_gain, queries, keys_values):
    per_group = MIXER_HEADS // GROUPS
    x_all = mixer_input.reshape(SEQUENCE_LENGTH, GROUPS, per_group, HEAD_P).transpose(1, 0, 2, 3)
    dt_all = jax.nn.softplus(step_raw).reshape(SEQUENCE_LENGTH, GROUPS, per_group).transpose(1, 0, 2)
    rates = (-jnp.exp(decay_log)).reshape(GROUPS, per_group)
    b_all = state_maps[:, 0].transpose(1, 0, 2)
    c_all = state_maps[:, 1].transpose(1, 0, 2)

    def one_group(inputs):
        x_rows, dt_rows, rate_row, b_rows, c_rows = inputs
        return span_pass(x_rows, dt_rows, rate_row, b_rows, c_rows)[0]
    mixed = lax.map(one_group, (x_all, dt_all, rates, b_all, c_all))
    mixed = mixed.transpose(1, 0, 2, 3).reshape(SEQUENCE_LENGTH, MIXER_HEADS, HEAD_P)
    mixed = mixed + skip_weight[None, :, None] * mixer_input.reshape(SEQUENCE_LENGTH, MIXER_HEADS, HEAD_P).astype(jnp.float32)
    gated = mixed * jax.nn.silu(gate_input.reshape(SEQUENCE_LENGTH, MIXER_HEADS, HEAD_P).astype(jnp.float32))
    grouped = gated.reshape(SEQUENCE_LENGTH, GROUPS, -1)
    mean_square = lax.optimization_barrier(jnp.mean(grouped * grouped, axis=2))
    normed = grouped * lax.rsqrt(mean_square + EPSILON)[:, :, None]
    mamba_out = (normed.reshape(SEQUENCE_LENGTH, -1) * norm_gain[None, :]).astype(jnp.bfloat16)
    per_kv = Q_HEADS // KV_HEADS
    query_heads = queries.reshape(SEQUENCE_LENGTH, Q_HEADS, ATT_HD).transpose(1, 0, 2)
    positions = jnp.arange(SEQUENCE_LENGTH)
    visible = positions[:, None] >= positions[None, :]

    def one_head(inputs):
        query_mat, head_index = inputs
        pair = lax.dynamic_index_in_dim(keys_values, head_index // per_kv, axis=2, keepdims=False)
        scores = jnp.dot(query_mat, pair[:, 0].T, preferred_element_type=jnp.float32) * ATT_HD ** (-0.5)
        scores = jnp.where(visible, scores, NEG_FILL)
        row_peak = lax.optimization_barrier(jnp.max(scores, axis=1, keepdims=True))
        weights = jnp.where(visible, jnp.exp(scores - row_peak), 0.0)
        totals = lax.optimization_barrier(jnp.sum(weights, axis=1))
        summed = jnp.dot(weights.astype(jnp.bfloat16), pair[:, 1], preferred_element_type=jnp.float32)
        return (summed / totals[:, None]).astype(jnp.bfloat16)
    attended = lax.map(one_head, (query_heads, jnp.arange(Q_HEADS, dtype=jnp.int32)))
    attn_out = attended.transpose(1, 0, 2).reshape(SEQUENCE_LENGTH, Q_HEADS * ATT_HD)
    return (mamba_out, attn_out)
```

```python
import functools
import math

import jax
import jax.numpy as jnp
from jax import lax
from jax.experimental import pallas as pl
from jax.experimental.pallas import tpu as pltpu
from jax.sharding import PartitionSpec as P

MESH = pl.DeviceIdType.MESH
HIGH = lax.Precision.HIGHEST
NEG_FILL = -1e30
EPSILON = 1e-5
SPAN = 128
CHUNKS = 4
UP = 8
DOWN = 7
M4_STEP = 4
M5_STEP = 7


def softplus(v):
    u = jnp.exp(-jnp.abs(v))
    small = u * (1.0 - u * (0.5 - u * (1.0 / 3.0 - u * 0.25)))
    return jnp.maximum(v, 0.0) + jnp.where(u < 0.02, small, jnp.log(1.0 + u))


def silu(v):
    return v / (1.0 + jnp.exp(-v))


def dot(a, b, **kw):
    return jnp.dot(a, b, preferred_element_type=jnp.float32, **kw)


def dot_t(a, b, **kw):
    return lax.dot_general(
        a, b, (((1,), (1,)), ((), ())), preferred_element_type=jnp.float32, **kw
    )


def kernel(
    n_ctx,
    decay_ref,
    skip_ref,
    step_ref,
    x_ref,
    gate_ref,
    maps_ref,
    gain_ref,
    q_ref,
    kv_ref,
    mamba_ref,
    attn_ref,
    kvbuf,
    qt,
    m_run,
    l_run,
    acc,
    mixed,
    decay_t,
    gated,
    total_buf,
    sbuf,
    srecv,
    ebuf,
    erecv,
    sq_buf,
    up_send,
    up_recv,
    dn_send,
    dn_recv,
    sib_send,
    sib_recv,
    sibd_send,
    sibd_recv,
    d_send,
    d_recv,
    s_send,
    s_recv,
    e_send,
    e_recv,
    q_send,
    q_recv,
):
    z = lax.axis_index("ctx")
    hd = lax.axis_index("head")
    core = lax.rem(hd, 2)
    sib = hd + 1 - 2 * core
    base = hd - lax.rem(hd, 4)
    place = lax.rem(hd, 4)
    above = lax.rem(z + 1, n_ctx)
    below = lax.rem(z + n_ctx - 1, n_ctx)

    barrier = pltpu.get_barrier_semaphore()

    def greet(d, carry):
        pl.semaphore_signal(
            barrier, inc=1, device_id=(lax.rem(z + d, n_ctx), hd), device_id_type=MESH
        )
        return carry

    lax.fori_loop(1, n_ctx, greet, 0)
    for d in range(1, 4):
        pl.semaphore_signal(
            barrier, inc=1, device_id=(z, base + lax.rem(place + d, 4)), device_id_type=MESH
        )

    for i in range(4):
        kvbuf[z, i] = kv_ref[0, i * 128 : (i + 1) * 128, :]
        kvbuf[z, 4 + i] = kv_ref[1, i * 128 : (i + 1) * 128, :].T
    for h in range(2):
        for i in range(4):
            qt[:, h * 512 + i * 128 : h * 512 + (i + 1) * 128] = q_ref[
                i * 128 : (i + 1) * 128, h * 128 : (h + 1) * 128
            ].T

    step = step_ref[...]
    raw = jnp.concatenate([step[:, k * SPAN : (k + 1) * SPAN] for k in range(4)], axis=0)
    row16 = lax.broadcasted_iota(jnp.int32, (16, SPAN), 0)
    rate = jnp.zeros((16, SPAN), jnp.float32)
    for h in range(4):
        rate = jnp.where(lax.rem(row16, 4) == h, decay_ref[h], rate)
    dt = softplus(raw)
    ell = -jnp.exp(rate) * dt
    upper = (
        lax.broadcasted_iota(jnp.int32, (SPAN, SPAN), 0)
        <= lax.broadcasted_iota(jnp.int32, (SPAN, SPAN), 1)
    ).astype(jnp.float32)
    cumul = dot(ell, upper, precision=HIGH)
    ends = cumul[:, SPAN - 1 : SPAN]
    tail = jnp.exp(ends - cumul) * dt
    offsets = [jnp.zeros((4, 1), jnp.float32)]
    for k in range(4):
        offsets.append(offsets[-1] + ends[k * 4 : (k + 1) * 4])
    from_start = cumul + jnp.concatenate(offsets[:4], axis=0)
    lane2 = lax.broadcasted_iota(jnp.int32, (2, 128), 1)
    total_rows = []
    for i in range(2):
        a = jnp.broadcast_to(offsets[4][2 * i : 2 * i + 1], (1, 128))
        b = jnp.broadcast_to(offsets[4][2 * i + 1 : 2 * i + 2], (1, 128))
        total_rows.append(jnp.where(lane2[0:1] < 64, a, b))
    total_buf[z] = jnp.concatenate(total_rows, axis=0)

    pl.semaphore_wait(barrier, n_ctx - 1 + 3)

    def up_copy(s, c):
        block = lax.rem(z - s + n_ctx, n_ctx)
        return pltpu.make_async_remote_copy(
            src_ref=kvbuf.at[block, core * 4 + c],
            dst_ref=kvbuf.at[block, core * 4 + c],
            send_sem=up_send.at[s * CHUNKS + c],
            recv_sem=up_recv.at[s * CHUNKS + c],
            device_id=(above, hd),
            device_id_type=MESH,
        )

    def down_copy(s, c):
        block = lax.rem(z + s, n_ctx)
        return pltpu.make_async_remote_copy(
            src_ref=kvbuf.at[block, core * 4 + c],
            dst_ref=kvbuf.at[block, core * 4 + c],
            send_sem=dn_send.at[s * CHUNKS + c],
            recv_sem=dn_recv.at[s * CHUNKS + c],
            device_id=(below, hd),
            device_id_type=MESH,
        )

    def up_arrival(s, c):
        block = lax.rem(z - s + n_ctx, n_ctx)
        return pltpu.make_async_remote_copy(
            src_ref=kvbuf.at[block, core * 4 + c],
            dst_ref=kvbuf.at[block, core * 4 + c],
            send_sem=up_send.at[(s - 1) * CHUNKS + c],
            recv_sem=up_recv.at[(s - 1) * CHUNKS + c],
            device_id=(above, hd),
            device_id_type=MESH,
        )

    def down_arrival(s, c):
        block = lax.rem(z + s, n_ctx)
        return pltpu.make_async_remote_copy(
            src_ref=kvbuf.at[block, core * 4 + c],
            dst_ref=kvbuf.at[block, core * 4 + c],
            send_sem=dn_send.at[(s - 1) * CHUNKS + c],
            recv_sem=dn_recv.at[(s - 1) * CHUNKS + c],
            device_id=(below, hd),
            device_id_type=MESH,
        )

    def sib_copy(block, part, send, recv, i):
        return pltpu.make_async_remote_copy(
            src_ref=kvbuf.at[block, part],
            dst_ref=kvbuf.at[block, part],
            send_sem=send.at[i],
            recv_sem=recv.at[i],
            device_id=(z, sib),
            device_id_type=MESH,
        )

    def up_block(s):
        return lax.rem(z - s + n_ctx, n_ctx)

    def down_block(s):
        return lax.rem(z + s, n_ctx)

    def travels_down(s):
        return lax.rem(z + s, n_ctx) <= n_ctx - 2 - UP

    def down_useful(s):
        return jnp.logical_and(z + s >= n_ctx, travels_down(s))

    for c in range(CHUNKS):

        @pl.when(z < n_ctx - 1)
        def _():
            up_copy(0, c).start()

        @pl.when(travels_down(0))
        def _():
            down_copy(0, c).start()

    def total_copy(d):
        return pltpu.make_async_remote_copy(
            src_ref=total_buf.at[z],
            dst_ref=total_buf.at[z],
            send_sem=d_send.at[d],
            recv_sem=d_recv.at[z],
            device_id=(lax.rem(z + d, n_ctx), hd),
            device_id_type=MESH,
        )

    def total_arrival(d):
        other = lax.rem(z + d, n_ctx)
        return pltpu.make_async_remote_copy(
            src_ref=total_buf.at[other],
            dst_ref=total_buf.at[other],
            send_sem=d_send.at[d],
            recv_sem=d_recv.at[other],
            device_id=(other, hd),
            device_id_type=MESH,
        )

    def state_copy(d):
        other = lax.rem(z + d, n_ctx)
        return pltpu.make_async_remote_copy(
            src_ref=sbuf.at[other],
            dst_ref=srecv.at[z],
            send_sem=s_send.at[d],
            recv_sem=s_recv.at[z],
            device_id=(other, hd),
            device_id_type=MESH,
        )

    def state_arrival(d):
        other = lax.rem(z + d, n_ctx)
        return pltpu.make_async_remote_copy(
            src_ref=sbuf.at[other],
            dst_ref=srecv.at[other],
            send_sem=s_send.at[d],
            recv_sem=s_recv.at[other],
            device_id=(other, hd),
            device_id_type=MESH,
        )

    def entering_copy(d):
        other = lax.rem(z + d, n_ctx)
        return pltpu.make_async_remote_copy(
            src_ref=ebuf.at[other],
            dst_ref=erecv.at[z],
            send_sem=e_send.at[d],
            recv_sem=e_recv.at[z],
            device_id=(other, hd),
            device_id_type=MESH,
        )

    def entering_arrival(d):
        other = lax.rem(z + d, n_ctx)
        return pltpu.make_async_remote_copy(
            src_ref=ebuf.at[other],
            dst_ref=erecv.at[other],
            send_sem=e_send.at[d],
            recv_sem=e_recv.at[other],
            device_id=(other, hd),
            device_id_type=MESH,
        )

    def each(first, last, action, cond=None):
        def turn(d, carry):
            if cond is None:
                action(d)
            else:

                @pl.when(cond(d))
                def _():
                    action(d)

            return carry

        lax.fori_loop(first, last, turn, 0)

    def other_of(d):
        return lax.rem(z + d, n_ctx)

    last = n_ctx - 1

    @pl.when(z < last)
    def _():
        each(1, n_ctx, lambda d: total_copy(d).start())

    row_r = lax.broadcasted_iota(jnp.int32, (16, 256), 0)
    head_l = lax.broadcasted_iota(jnp.int32, (16, 256), 1) // 64
    tail_t, cumul_t, start_t = tail.T, cumul.T, from_start.T
    running = None
    run_list = []
    for k in range(4):
        rows = slice(k * SPAN, (k + 1) * SPAN)
        pick = (row_r == k * 4 + head_l).astype(jnp.float32)
        tail_x = dot(tail_t, pick, precision=HIGH)
        decay_t[rows, :] = jnp.exp(dot(start_t, pick, precision=HIGH))
        loads = (x_ref[rows, :].astype(jnp.float32) * tail_x).astype(jnp.bfloat16)
        fresh = dot(maps_ref[0, rows, :].T, loads)
        end_lane = jnp.sum(jnp.broadcast_to(ends, (16, 256)) * pick, axis=0, keepdims=True)
        running = fresh if k == 0 else jnp.exp(end_lane) * running + fresh
        run_list.append(running)
    for i in range(n_ctx):
        half, r = i // 8, i % 8
        sbuf[i] = running[r * 16 : (r + 1) * 16, half * 128 : (half + 1) * 128].astype(
            jnp.bfloat16
        )

    @pl.when(z < last)
    def _():
        each(1, n_ctx, lambda d: state_copy(d).start())

    lane_w = lax.broadcasted_iota(jnp.int32, (SPAN, SPAN), 1)
    below_diag = lax.broadcasted_iota(jnp.int32, (SPAN, SPAN), 0) >= lane_w
    lane_p = lax.broadcasted_iota(jnp.int32, (1, 256), 1) // 64
    skip = jnp.zeros((1, 256), jnp.float32)
    for h in range(4):
        skip = jnp.where(lane_p == h, skip_ref[h], skip)
    left = lane_w < 64
    for k in range(4):
        rows = slice(k * SPAN, (k + 1) * SPAN)
        b_mat, c_mat = maps_ref[0, rows, :], maps_ref[1, rows, :]
        scores = dot_t(c_mat, b_mat)
        for pair in range(2):
            lanes = slice(pair * 128, (pair + 1) * 128)
            x_pair = x_ref[rows, lanes]
            weights = []
            for h in (2 * pair, 2 * pair + 1):
                r = k * 4 + h
                spread = cumul_t[:, r : r + 1] - cumul[r : r + 1, :]
                grown = jnp.exp(jnp.where(below_diag, spread, NEG_FILL))
                weights.append((scores * grown * dt[r : r + 1, :]).astype(jnp.bfloat16))
            zero = jnp.zeros_like(x_pair)
            x_two = jnp.concatenate(
                [jnp.where(left, x_pair, zero), jnp.where(left, zero, x_pair)], axis=0
            )
            inside = dot(jnp.concatenate(weights, axis=1), x_two)
            total = inside + skip[:, lanes] * x_pair.astype(jnp.float32)
            mixed[rows, lanes] = total
        if k > 0:
            pick = (row_r == k * 4 + head_l).astype(jnp.float32)
            grown_in = jnp.exp(dot(cumul_t, pick, precision=HIGH))
            mixed[rows, :] += dot(c_mat, run_list[k - 1].astype(jnp.bfloat16)) * grown_in

    coef = math.log2(math.e) / math.sqrt(128.0)

    def diagonal(t):
        lanes = slice(t * 128, (t + 1) * 128)
        tile = t % 4
        count = (tile + 1) * 128
        k_mat = kvbuf[z, 0 : tile + 1].reshape(count, 128)
        s = dot(k_mat, qt[:, lanes])
        key = lax.broadcasted_iota(jnp.int32, (count, 128), 0)
        query = lax.broadcasted_iota(jnp.int32, (count, 128), 1) + tile * 128
        s = jnp.where(key <= query, s, NEG_FILL)
        m = jnp.max(s, axis=0, keepdims=True)
        p = jnp.exp2((s - m) * coef)
        m_run[:, lanes] = m
        l_run[:, lanes] = jnp.sum(p, axis=0, keepdims=True)
        v_mat = jnp.concatenate([kvbuf[z, 4 + i] for i in range(tile + 1)], axis=1)
        acc[:, lanes] = dot(v_mat, p.astype(jnp.bfloat16))

    def attend(block, t):
        lanes = slice(t * 128, (t + 1) * 128)
        s = dot(kvbuf[block, 0:4].reshape(512, 128), qt[:, lanes])
        before = m_run[:, lanes]
        m = jnp.maximum(before, jnp.max(s, axis=0, keepdims=True))
        p = jnp.exp2((s - m) * coef)
        scale = jnp.exp2((before - m) * coef)
        m_run[:, lanes] = m
        l_run[:, lanes] = l_run[:, lanes] * scale + jnp.sum(p, axis=0, keepdims=True)
        v_mat = jnp.concatenate([kvbuf[block, 4 + i] for i in range(4)], axis=1)
        acc[:, lanes] = acc[:, lanes] * scale + dot(v_mat, p.astype(jnp.bfloat16))

    for t in range(8):
        diagonal(t)

    def prefix():
        each(
            1,
            n_ctx,
            lambda d: (total_arrival(d).wait_recv(), state_arrival(d).wait_recv()),
            lambda d: other_of(d) < last,
        )
        srecv[z] = sbuf[z]
        half = z // 8
        entering = jnp.zeros((16, 128), jnp.float32)
        for k in range(n_ctx):
            ebuf[k] = entering.astype(jnp.bfloat16)
            if k < last:
                entering = (
                    jnp.exp(total_buf[k, pl.ds(half, 1), :]) * entering
                    + srecv[k].astype(jnp.float32)
                )
        erecv[z] = ebuf[z]
        each(1, n_ctx, lambda d: entering_copy(d).start(), lambda d: other_of(d) > 0)

    def finish_mixed():
        @pl.when(z > 0)
        def _():
            each(1, n_ctx, lambda d: entering_arrival(d).wait_recv())
            e_mat = [erecv[i * 8 : (i + 1) * 8].reshape(128, 128) for i in range(2)]
            for k in range(4):
                rows = slice(k * SPAN, (k + 1) * SPAN)
                for i in range(2):
                    lanes = slice(i * 128, (i + 1) * 128)
                    mixed[rows, lanes] += dot(maps_ref[1, rows, :], e_mat[i]) * decay_t[rows, lanes]

        ones = jnp.ones((8, 256), jnp.bfloat16)
        for k in range(4):
            rows = slice(k * SPAN, (k + 1) * SPAN)
            value = mixed[rows, :] * silu(gate_ref[rows, :].astype(jnp.float32))
            gated[rows, :] = value
            squares = (value * value).astype(jnp.bfloat16)
            sq_buf[place, :, k * SPAN : (k + 1) * SPAN] = dot_t(ones, squares)
        for d in range(1, 4):
            square_copy(d).start()

    def square_copy(d):
        return pltpu.make_async_remote_copy(
            src_ref=sq_buf.at[place],
            dst_ref=sq_buf.at[place],
            send_sem=q_send.at[d],
            recv_sem=q_recv.at[place],
            device_id=(z, base + lax.rem(place + d, 4)),
            device_id_type=MESH,
        )

    def square_arrival(d):
        other = lax.rem(place + d, 4)
        return pltpu.make_async_remote_copy(
            src_ref=sq_buf.at[other],
            dst_ref=sq_buf.at[other],
            send_sem=q_send.at[d],
            recv_sem=q_recv.at[other],
            device_id=(z, base + other),
            device_id_type=MESH,
        )

    def finish_norm():
        for d in range(1, 4):
            square_arrival(d).wait_recv()
        total = sq_buf[0] + sq_buf[1] + sq_buf[2] + sq_buf[3]
        inv = lax.rsqrt(total * (1.0 / 1024.0) + EPSILON)
        row8 = lax.broadcasted_iota(jnp.int32, (8, 256), 0)
        gain = jnp.broadcast_to(gain_ref[...].reshape(1, 256), (8, 256))
        gain = jnp.where(row8 == 0, gain, 0.0)
        for k in range(4):
            rows = slice(k * SPAN, (k + 1) * SPAN)
            factor = dot(inv[:, k * SPAN : (k + 1) * SPAN].T, gain, precision=HIGH)
            mamba_ref[rows, :] = (gated[rows, :] * factor).astype(jnp.bfloat16)

    def ring(s, carry):
        for c in range(CHUNKS):

            @pl.when(z >= s)
            def _():
                up_arrival(s, c).wait_recv()

                @pl.when(jnp.logical_and(z < last, s < UP))
                def _():
                    up_copy(s, c).start()

                sib_copy(up_block(s), core * 4 + c, sib_send, sib_recv, s * CHUNKS + c).start()

            @pl.when(jnp.logical_and(s <= DOWN, travels_down(s)))
            def _():
                down_arrival(s, c).wait_recv()

                @pl.when(s < DOWN)
                def _():
                    down_copy(s, c).start()

                @pl.when(z + s >= n_ctx)
                def _():
                    sib_copy(
                        down_block(s), core * 4 + c, sibd_send, sibd_recv, s * CHUNKS + c
                    ).start()

            if c == 0:
                sib_wait(s - 1)
            attend_two(s - 1, c)

        @pl.when(s == M4_STEP)
        def _():
            prefix()

        @pl.when(s == M5_STEP)
        def _():
            finish_mixed()

        return carry

    def sib_wait(s):
        @pl.when(jnp.logical_and(s >= 1, z >= s))
        def _():
            for c in range(CHUNKS):
                sib_copy(
                    up_block(s), (1 - core) * 4 + c, sib_send, sib_recv, s * CHUNKS + c
                ).wait_recv()

        @pl.when(jnp.logical_and(jnp.logical_and(s >= 1, s <= DOWN), down_useful(s)))
        def _():
            for c in range(CHUNKS):
                sib_copy(
                    down_block(s), (1 - core) * 4 + c, sibd_send, sibd_recv, s * CHUNKS + c
                ).wait_recv()

    def attend_two(s, c):
        @pl.when(jnp.logical_and(s >= 1, z >= s))
        def _():
            attend(up_block(s), 2 * c)
            attend(up_block(s), 2 * c + 1)

        @pl.when(jnp.logical_and(jnp.logical_and(s >= 1, s <= DOWN), down_useful(s)))
        def _():
            attend(down_block(s), 2 * c)
            attend(down_block(s), 2 * c + 1)

    lax.fori_loop(1, UP + 1, ring, 0)
    sib_wait(UP)

    @pl.when(z >= UP)
    def _():
        for t in range(8):
            attend(up_block(UP), t)

    finish_norm()
    for h in range(2):
        for i in range(4):
            lanes = slice(h * 512 + i * 128, h * 512 + (i + 1) * 128)
            result = acc[:, lanes] / l_run[:, lanes]
            attn_ref[i * 128 : (i + 1) * 128, h * 128 : (h + 1) * 128] = result.T.astype(
                jnp.bfloat16
            )

    def sent(s, carry):
        for c in range(CHUNKS):

            @pl.when(jnp.logical_and(z >= s, z < last))
            def _():
                up_copy(s, c).wait_send()

            @pl.when(jnp.logical_and(s < DOWN, travels_down(s)))
            def _():
                down_copy(s, c).wait_send()

        return carry

    def sent_sib(s, carry):
        for c in range(CHUNKS):

            @pl.when(z >= s)
            def _():
                sib_copy(up_block(s), core * 4 + c, sib_send, sib_recv, s * CHUNKS + c).wait_send()

            @pl.when(jnp.logical_and(s <= DOWN, down_useful(s)))
            def _():
                sib_copy(
                    down_block(s), core * 4 + c, sibd_send, sibd_recv, s * CHUNKS + c
                ).wait_send()

        return carry

    lax.fori_loop(0, UP, sent, 0)
    lax.fori_loop(1, UP + 1, sent_sib, 0)

    @pl.when(z < last)
    def _():
        each(1, n_ctx, lambda d: (total_copy(d).wait_send(), state_copy(d).wait_send()))

    each(1, n_ctx, lambda d: entering_copy(d).wait_send(), lambda d: other_of(d) > 0)
    for d in range(1, 4):
        square_copy(d).wait_send()


def body(
    n_ctx,
    mixer_input,
    gate_input,
    step_raw,
    decay_log,
    skip_weight,
    state_maps,
    norm_gain,
    queries,
    keys_values,
):
    group = lax.axis_index("head") // 4
    maps = lax.dynamic_index_in_dim(state_maps, group, axis=2, keepdims=False)
    pairs = lax.dynamic_index_in_dim(keys_values, group, axis=2, keepdims=False)
    maps = maps.transpose(1, 0, 2)
    pairs = pairs.transpose(1, 0, 2)
    vmem = pl.BlockSpec(memory_space=pltpu.VMEM)
    smem = pl.BlockSpec(memory_space=pltpu.SMEM)
    dma = pltpu.SemaphoreType.DMA
    rows = mixer_input.shape[0]
    return pl.pallas_call(
        functools.partial(kernel, n_ctx),
        out_shape=(
            jax.ShapeDtypeStruct((rows, 256), jnp.bfloat16),
            jax.ShapeDtypeStruct((rows, 256), jnp.bfloat16),
        ),
        in_specs=[smem, smem] + [vmem] * 7,
        out_specs=(vmem, vmem),
        scratch_shapes=[
            pltpu.VMEM((n_ctx, 8, 128, 128), jnp.bfloat16),
            pltpu.VMEM((128, 1024), jnp.bfloat16),
            pltpu.VMEM((1, 1024), jnp.float32),
            pltpu.VMEM((1, 1024), jnp.float32),
            pltpu.VMEM((128, 1024), jnp.float32),
            pltpu.VMEM((512, 256), jnp.float32),
            pltpu.VMEM((512, 256), jnp.float32),
            pltpu.VMEM((512, 256), jnp.float32),
            pltpu.VMEM((n_ctx, 2, 128), jnp.float32),
            pltpu.VMEM((n_ctx, 16, 128), jnp.bfloat16),
            pltpu.VMEM((n_ctx, 16, 128), jnp.bfloat16),
            pltpu.VMEM((n_ctx, 16, 128), jnp.bfloat16),
            pltpu.VMEM((n_ctx, 16, 128), jnp.bfloat16),
            pltpu.VMEM((4, 8, 512), jnp.float32),
            dma((UP * CHUNKS,)),
            dma((UP * CHUNKS,)),
            dma((DOWN * CHUNKS,)),
            dma((DOWN * CHUNKS,)),
            dma(((UP + 1) * CHUNKS,)),
            dma(((UP + 1) * CHUNKS,)),
            dma(((DOWN + 1) * CHUNKS,)),
            dma(((DOWN + 1) * CHUNKS,)),
            dma((n_ctx,)),
            dma((n_ctx,)),
            dma((n_ctx,)),
            dma((n_ctx,)),
            dma((n_ctx,)),
            dma((n_ctx,)),
            dma((4,)),
            dma((4,)),
        ],
        compiler_params=pltpu.CompilerParams(
            collective_id=0, has_side_effects=True, vmem_limit_bytes=40 * 2**20
        ),
    )(
        decay_log,
        skip_weight,
        step_raw.T,
        mixer_input,
        gate_input,
        maps,
        norm_gain,
        queries,
        pairs,
    )


def solution(mesh):
    in_specs = (
        P("ctx", "head"),
        P("ctx", "head"),
        P("ctx", "head"),
        P("head"),
        P("head"),
        P("ctx", None, None, None),
        P("head"),
        P("ctx", "head"),
        P("ctx", None, None, None),
    )
    return jax.shard_map(
        functools.partial(body, mesh.shape["ctx"]),
        mesh=mesh,
        in_specs=in_specs,
        out_specs=(P("ctx", "head"), P("ctx", "head")),
        check_vma=False,
    )
```

```python
import functools
import math

import jax
import jax.numpy as jnp
from jax import lax
from jax.experimental import pallas as pl
from jax.experimental.pallas import tpu as pltpu
from jax.sharding import PartitionSpec as P

MESH = pl.DeviceIdType.MESH
HIGH = lax.Precision.HIGHEST
NEG_FILL = -1e30
EPSILON = 1e-5
SPAN = 128
CHUNKS = 4
UP = 8
HALF = CHUNKS // 2
NEAR = 2
STATE_STEP = 1
M4_STEP = 4
M5_STEP = 7


def softplus(v):
    u = jnp.exp(-jnp.abs(v))
    small = u * (1.0 - u * (0.5 - u * (1.0 / 3.0 - u * 0.25)))
    return jnp.maximum(v, 0.0) + jnp.where(u < 0.02, small, jnp.log(1.0 + u))


def silu(v):
    return v / (1.0 + jnp.exp(-v))


def dot(a, b, **kw):
    return jnp.dot(a, b, preferred_element_type=jnp.float32, **kw)


def parts_of(v):
    high = v.astype(jnp.bfloat16)
    rest = v - high.astype(jnp.float32)
    middle = rest.astype(jnp.bfloat16)
    low = (rest - middle.astype(jnp.float32)).astype(jnp.bfloat16)
    return high, middle, low


def dot_t(a, b, **kw):
    return lax.dot_general(
        a, b, (((1,), (1,)), ((), ())), preferred_element_type=jnp.float32, **kw
    )


def kernel(
    n_ctx,
    decay_ref,
    skip_ref,
    step_ref,
    gain_ref,
    x_hbm,
    gate_hbm,
    maps_hbm,
    q_hbm,
    kv_hbm,
    mamba_ref,
    attn_ref,
    x_ref,
    gate_ref,
    q_ref,
    maps_raw,
    kv_raw,
    wide,
    maps_ref,
    in_sem,
    far_sem,
    kvbuf,
    qt,
    m_run,
    l_run,
    acc,
    mixed,
    decay_t,
    gated,
    total_buf,
    sbuf,
    srecv,
    ebuf,
    erecv,
    sq_buf,
    up_send,
    up_recv,
    dn_send,
    dn_recv,
    sib_send,
    sib_recv,
    sibd_send,
    sibd_recv,
    d_send,
    d_recv,
    s_send,
    s_recv,
    e_send,
    e_recv,
    q_send,
    q_recv,
):
    z = lax.axis_index("ctx")
    hd = lax.axis_index("head")
    core = lax.rem(hd, 2)
    sib = hd + 1 - 2 * core
    base = hd - lax.rem(hd, 4)
    place = lax.rem(hd, 4)
    above = lax.rem(z + 1, n_ctx)
    below = lax.rem(z + n_ctx - 1, n_ctx)

    barrier = pltpu.get_barrier_semaphore()
    for d in range(NEAR, 0, -1):
        for other in (lax.rem(z + d, n_ctx), lax.rem(z + n_ctx - d, n_ctx)):
            pl.semaphore_signal(barrier, inc=1, device_id=(other, hd), device_id_type=MESH)
    for d in range(1, 4):
        pl.semaphore_signal(
            barrier, inc=1, device_id=(z, base + lax.rem(place + d, 4)), device_id_type=MESH
        )

    fetches = []
    for src, dst in ((kv_hbm, kv_raw), (maps_hbm, maps_raw)):
        for rows in (pl.ds(0, 4096), pl.ds(4096, 4096)):
            fetches.append((src.at[rows], dst.at[rows]))
    fetches += [(q_hbm, q_ref), (x_hbm, x_ref), (gate_hbm, gate_ref)]
    fetches = [
        pltpu.make_async_copy(src, dst, in_sem.at[i]) for i, (src, dst) in enumerate(fetches)
    ]
    for fetch in fetches:
        fetch.start()

    def pick_group(raw, waits):
        for i, fetch in enumerate(waits):
            fetch.wait()

            def widen(k, carry):
                rows = pl.ds(pl.multiple_of(i * 4096 + k * 512, 512), 512)
                wide[rows, :] = raw[rows, :].astype(jnp.float32)
                return carry

            lax.fori_loop(0, 8, widen, 0)
        return [wide[pl.ds(8 * i + hd // 4, 512, stride=16), :] for i in range(2)]

    keys, values = pick_group(kv_raw, fetches[0:2])
    for i in range(4):
        kvbuf[z, i] = keys[i * 128 : (i + 1) * 128, :].astype(jnp.bfloat16)
        kvbuf[z, 4 + i] = values[i * 128 : (i + 1) * 128, :].T.astype(jnp.bfloat16)

    step = step_ref[...]
    raw = jnp.concatenate([step[:, k * SPAN : (k + 1) * SPAN] for k in range(4)], axis=0)
    row16 = lax.broadcasted_iota(jnp.int32, (16, SPAN), 0)
    rate = jnp.zeros((16, SPAN), jnp.float32)
    for h in range(4):
        rate = jnp.where(lax.rem(row16, 4) == h, decay_ref[h], rate)
    dt = softplus(raw)
    ell = -jnp.exp(rate) * dt
    upper = (
        lax.broadcasted_iota(jnp.int32, (SPAN, SPAN), 0)
        <= lax.broadcasted_iota(jnp.int32, (SPAN, SPAN), 1)
    ).astype(jnp.float32)
    cumul = dot(ell, upper, precision=HIGH)
    ends = cumul[:, SPAN - 1 : SPAN]
    tail = jnp.exp(ends - cumul) * dt
    offsets = [jnp.zeros((4, 1), jnp.float32)]
    for k in range(4):
        offsets.append(offsets[-1] + ends[k * 4 : (k + 1) * 4])
    from_start = cumul + jnp.concatenate(offsets[:4], axis=0)
    lane2 = lax.broadcasted_iota(jnp.int32, (2, 128), 1)
    total_rows = []
    for i in range(2):
        a = jnp.broadcast_to(offsets[4][2 * i : 2 * i + 1], (1, 128))
        b = jnp.broadcast_to(offsets[4][2 * i + 1 : 2 * i + 2], (1, 128))
        total_rows.append(jnp.where(lane2[0:1] < 64, a, b))
    total_buf[z] = jnp.concatenate(total_rows, axis=0)

    def up_copy(s, c):
        block = lax.rem(z - s + n_ctx, n_ctx)
        return pltpu.make_async_remote_copy(
            src_ref=kvbuf.at[block, core * 4 + c],
            dst_ref=kvbuf.at[block, core * 4 + c],
            send_sem=up_send.at[s * CHUNKS + c],
            recv_sem=up_recv.at[s * CHUNKS + c],
            device_id=(above, hd),
            device_id_type=MESH,
        )

    def down_copy(s, c):
        block = lax.rem(z + s, n_ctx)
        return pltpu.make_async_remote_copy(
            src_ref=kvbuf.at[block, core * 4 + c],
            dst_ref=kvbuf.at[block, core * 4 + c],
            send_sem=dn_send.at[s * CHUNKS + c],
            recv_sem=dn_recv.at[s * CHUNKS + c],
            device_id=(below, hd),
            device_id_type=MESH,
        )

    def up_arrival(s, c):
        block = lax.rem(z - s + n_ctx, n_ctx)
        return pltpu.make_async_remote_copy(
            src_ref=kvbuf.at[block, core * 4 + c],
            dst_ref=kvbuf.at[block, core * 4 + c],
            send_sem=up_send.at[(s - 1) * CHUNKS + c],
            recv_sem=up_recv.at[(s - 1) * CHUNKS + c],
            device_id=(above, hd),
            device_id_type=MESH,
        )

    def down_arrival(s, c):
        block = lax.rem(z + s, n_ctx)
        return pltpu.make_async_remote_copy(
            src_ref=kvbuf.at[block, core * 4 + c],
            dst_ref=kvbuf.at[block, core * 4 + c],
            send_sem=dn_send.at[(s - 1) * CHUNKS + c],
            recv_sem=dn_recv.at[(s - 1) * CHUNKS + c],
            device_id=(below, hd),
            device_id_type=MESH,
        )

    def sib_copy(block, part, send, recv, i):
        return pltpu.make_async_remote_copy(
            src_ref=kvbuf.at[block, part],
            dst_ref=kvbuf.at[block, part],
            send_sem=send.at[i],
            recv_sem=recv.at[i],
            device_id=(z, sib),
            device_id_type=MESH,
        )

    def up_block(s):
        return lax.rem(z - s + n_ctx, n_ctx)

    def down_block(s):
        return lax.rem(z + s, n_ctx)

    def up_hops(c):
        return UP if c < HALF else UP - 1

    def down_hops(c):
        return UP - 1 if c < HALF else UP

    def came_up(s, c):
        return jnp.logical_and(z >= s, s <= up_hops(c))

    def travels_down(s, c):
        block = lax.rem(z + s, n_ctx)
        return jnp.logical_and(block < down_hops(c), s <= down_hops(c))

    def down_useful(s, c):
        return jnp.logical_and(z + s >= n_ctx, travels_down(s, c))

    def total_copy(d):
        return pltpu.make_async_remote_copy(
            src_ref=total_buf.at[z],
            dst_ref=total_buf.at[z],
            send_sem=d_send.at[d],
            recv_sem=d_recv.at[z],
            device_id=(lax.rem(z + d, n_ctx), hd),
            device_id_type=MESH,
        )

    def total_arrival(d):
        other = lax.rem(z + d, n_ctx)
        return pltpu.make_async_remote_copy(
            src_ref=total_buf.at[other],
            dst_ref=total_buf.at[other],
            send_sem=d_send.at[d],
            recv_sem=d_recv.at[other],
            device_id=(other, hd),
            device_id_type=MESH,
        )

    def state_copy(d):
        other = lax.rem(z + d, n_ctx)
        return pltpu.make_async_remote_copy(
            src_ref=sbuf.at[other],
            dst_ref=srecv.at[z],
            send_sem=s_send.at[d],
            recv_sem=s_recv.at[z],
            device_id=(other, hd),
            device_id_type=MESH,
        )

    def state_arrival(d):
        other = lax.rem(z + d, n_ctx)
        return pltpu.make_async_remote_copy(
            src_ref=sbuf.at[other],
            dst_ref=srecv.at[other],
            send_sem=s_send.at[d],
            recv_sem=s_recv.at[other],
            device_id=(other, hd),
            device_id_type=MESH,
        )

    def entering_copy(d):
        other = lax.rem(z + d, n_ctx)
        return pltpu.make_async_remote_copy(
            src_ref=ebuf.at[other],
            dst_ref=erecv.at[z],
            send_sem=e_send.at[d],
            recv_sem=e_recv.at[z],
            device_id=(other, hd),
            device_id_type=MESH,
        )

    def entering_arrival(d):
        other = lax.rem(z + d, n_ctx)
        return pltpu.make_async_remote_copy(
            src_ref=ebuf.at[other],
            dst_ref=erecv.at[other],
            send_sem=e_send.at[d],
            recv_sem=e_recv.at[other],
            device_id=(other, hd),
            device_id_type=MESH,
        )

    def each(first, last, action, cond=None):
        def turn(d, carry):
            if cond is None:
                action(d)
            else:

                @pl.when(cond(d))
                def _():
                    action(d)

            return carry

        lax.fori_loop(first, last, turn, 0)

    def other_of(d):
        return lax.rem(z + d, n_ctx)

    last = n_ctx - 1

    b_all, c_all = pick_group(maps_raw, fetches[2:4])
    maps_ref[0] = b_all.astype(jnp.bfloat16)
    maps_ref[1] = c_all.astype(jnp.bfloat16)
    fetches[5].wait()
    row_r = lax.broadcasted_iota(jnp.int32, (16, 256), 0)
    head_l = lax.broadcasted_iota(jnp.int32, (16, 256), 1) // 64
    tail_t, start_t = (jnp.concatenate(parts_of(v.T), axis=1) for v in (tail, from_start))
    cumul_t = cumul.T
    cumul_3 = jnp.concatenate(parts_of(cumul_t), axis=1)
    running = None
    run_list = []
    for k in range(4):
        rows = slice(k * SPAN, (k + 1) * SPAN)
        pick = (row_r == k * 4 + head_l).astype(jnp.float32)
        pick_3 = jnp.concatenate([pick.astype(jnp.bfloat16)] * 3, axis=0)
        tail_x = dot(tail_t, pick_3)
        decay_t[rows, :] = jnp.exp(dot(start_t, pick_3))
        loads = (x_ref[rows, :].astype(jnp.float32) * tail_x).astype(jnp.bfloat16)
        fresh = dot(maps_ref[0, rows, :].T, loads)
        end_lane = jnp.sum(jnp.broadcast_to(ends, (16, 256)) * pick, axis=0, keepdims=True)
        running = fresh if k == 0 else jnp.exp(end_lane) * running + fresh
        run_list.append(running)
    for i in range(n_ctx):
        half, r = i // 8, i % 8
        sbuf[i] = running[r * 16 : (r + 1) * 16, half * 128 : (half + 1) * 128].astype(
            jnp.bfloat16
        )

    fetches[4].wait()
    for h in range(2):
        for i in range(4):
            qt[:, h * 512 + i * 128 : h * 512 + (i + 1) * 128] = q_ref[
                i * 128 : (i + 1) * 128, h * 128 : (h + 1) * 128
            ].T

    pl.semaphore_wait(barrier, 2 * NEAR + 3)
    for c in range(CHUNKS):

        @pl.when(z < n_ctx - 1)
        def _():
            up_copy(0, c).start()

        @pl.when(travels_down(0, c))
        def _():
            down_copy(0, c).start()

    def tell(i):
        d = NEAR * 2**i
        for other in (lax.rem(z + d, n_ctx), lax.rem(z + n_ctx - d, n_ctx)):
            pl.semaphore_signal(far_sem.at[i], inc=1, device_id=(other, hd), device_id_type=MESH)

    tell(0)

    def send_states():
        pl.semaphore_wait(far_sem.at[1], 2)

        @pl.when(z < last)
        def _():
            each(1, n_ctx, lambda d: (total_copy(d).start(), state_copy(d).start()))

    lane_w = lax.broadcasted_iota(jnp.int32, (SPAN, SPAN), 1)
    below_diag = lax.broadcasted_iota(jnp.int32, (SPAN, SPAN), 0) >= lane_w
    lane_p = lax.broadcasted_iota(jnp.int32, (1, 256), 1) // 64
    skip = jnp.zeros((1, 256), jnp.float32)
    for h in range(4):
        skip = jnp.where(lane_p == h, skip_ref[h], skip)
    left = lane_w < 64
    for k in range(4):
        rows = slice(k * SPAN, (k + 1) * SPAN)
        b_mat, c_mat = maps_ref[0, rows, :], maps_ref[1, rows, :]
        scores = dot_t(c_mat, b_mat)
        for pair in range(2):
            lanes = slice(pair * 128, (pair + 1) * 128)
            x_pair = x_ref[rows, lanes]
            weights = []
            for h in (2 * pair, 2 * pair + 1):
                r = k * 4 + h
                spread = cumul_t[:, r : r + 1] - cumul[r : r + 1, :]
                grown = jnp.exp(jnp.where(below_diag, spread, NEG_FILL))
                weights.append((scores * grown * dt[r : r + 1, :]).astype(jnp.bfloat16))
            zero = jnp.zeros_like(x_pair)
            x_two = jnp.concatenate(
                [jnp.where(left, x_pair, zero), jnp.where(left, zero, x_pair)], axis=0
            )
            inside = dot(jnp.concatenate(weights, axis=1), x_two)
            total = inside + skip[:, lanes] * x_pair.astype(jnp.float32)
            mixed[rows, lanes] = total
        if k > 0:
            pick = (row_r == k * 4 + head_l).astype(jnp.bfloat16)
            grown_in = jnp.exp(dot(cumul_3, jnp.concatenate([pick] * 3, axis=0)))
            mixed[rows, :] += dot(c_mat, run_list[k - 1].astype(jnp.bfloat16)) * grown_in

    coef = math.log2(math.e) / math.sqrt(128.0)

    def diagonal(t):
        lanes = slice(t * 128, (t + 1) * 128)
        tile = t % 4
        count = (tile + 1) * 128
        k_mat = kvbuf[z, 0 : tile + 1].reshape(count, 128)
        s = dot(k_mat, qt[:, lanes])
        key = lax.broadcasted_iota(jnp.int32, (count, 128), 0)
        query = lax.broadcasted_iota(jnp.int32, (count, 128), 1) + tile * 128
        s = jnp.where(key <= query, s, NEG_FILL)
        m = jnp.max(s, axis=0, keepdims=True)
        p = jnp.exp2((s - m) * coef)
        m_run[:, lanes] = m
        l_run[:, lanes] = jnp.sum(p, axis=0, keepdims=True)
        v_mat = jnp.concatenate([kvbuf[z, 4 + i] for i in range(tile + 1)], axis=1)
        acc[:, lanes] = dot(v_mat, p.astype(jnp.bfloat16))

    ones = jnp.ones((16, 256), jnp.bfloat16)

    def attend(blocks, t):
        lanes = slice(t * 256, (t + 1) * 256)
        queries = qt[:, lanes]
        parts = [(b, i) for b in blocks for i in range(2)]
        scores = [dot(kvbuf[b, 2 * i : 2 * i + 2].reshape(256, 128), queries) for b, i in parts]
        before = m_run[:, lanes]
        m = before
        for s in scores:
            m = jnp.maximum(m, jnp.max(s, axis=0, keepdims=True))
        scale = jnp.exp2((before - m) * coef)
        m_run[:, lanes] = m
        summed = None
        for (b, i), s in zip(parts, scores):
            p = jnp.exp2((s - m) * coef).astype(jnp.bfloat16)
            v_mat = jnp.concatenate([kvbuf[b, 4 + 2 * i], kvbuf[b, 5 + 2 * i]], axis=1)
            part = dot(jnp.concatenate([v_mat, ones], axis=0), p)
            summed = part if summed is None else summed + part
        l_run[:, lanes] = l_run[:, lanes] * scale + summed[128:129]
        acc[:, lanes] = acc[:, lanes] * scale + summed[0:128]

    for t in range(8):
        diagonal(t)

    def prefix():
        each(
            1,
            n_ctx,
            lambda d: (total_arrival(d).wait_recv(), state_arrival(d).wait_recv()),
            lambda d: other_of(d) < last,
        )
        srecv[z] = sbuf[z]
        half = z // 8
        entering = jnp.zeros((16, 128), jnp.float32)
        for k in range(n_ctx):
            ebuf[k] = entering.astype(jnp.bfloat16)
            if k < last:
                entering = (
                    jnp.exp(total_buf[k, pl.ds(half, 1), :]) * entering
                    + srecv[k].astype(jnp.float32)
                )
        erecv[z] = ebuf[z]
        each(1, n_ctx, lambda d: entering_copy(d).start(), lambda d: other_of(d) > 0)

    def finish_mixed():
        @pl.when(z > 0)
        def _():
            each(1, n_ctx, lambda d: entering_arrival(d).wait_recv())
            e_mat = [erecv[i * 8 : (i + 1) * 8].reshape(128, 128) for i in range(2)]
            for k in range(4):
                rows = slice(k * SPAN, (k + 1) * SPAN)
                for i in range(2):
                    lanes = slice(i * 128, (i + 1) * 128)
                    mixed[rows, lanes] += dot(maps_ref[1, rows, :], e_mat[i]) * decay_t[rows, lanes]

        ones8 = jnp.ones((8, 256), jnp.bfloat16)
        fetches[6].wait()
        for k in range(4):
            rows = slice(k * SPAN, (k + 1) * SPAN)
            value = mixed[rows, :] * silu(gate_ref[rows, :].astype(jnp.float32))
            gated[rows, :] = value
            squares = (value * value).astype(jnp.bfloat16)
            sq_buf[place, :, k * SPAN : (k + 1) * SPAN] = dot_t(ones8, squares)
        for d in range(1, 4):
            square_copy(d).start()

    def square_copy(d):
        return pltpu.make_async_remote_copy(
            src_ref=sq_buf.at[place],
            dst_ref=sq_buf.at[place],
            send_sem=q_send.at[d],
            recv_sem=q_recv.at[place],
            device_id=(z, base + lax.rem(place + d, 4)),
            device_id_type=MESH,
        )

    def square_arrival(d):
        other = lax.rem(place + d, 4)
        return pltpu.make_async_remote_copy(
            src_ref=sq_buf.at[other],
            dst_ref=sq_buf.at[other],
            send_sem=q_send.at[d],
            recv_sem=q_recv.at[other],
            device_id=(z, base + other),
            device_id_type=MESH,
        )

    def finish_norm():
        for d in range(1, 4):
            square_arrival(d).wait_recv()
        total = sq_buf[0] + sq_buf[1] + sq_buf[2] + sq_buf[3]
        inv = lax.rsqrt(total * (1.0 / 1024.0) + EPSILON)
        i_parts = [v[0:1] for v in parts_of(inv)]
        g_parts = parts_of(gain_ref[...].reshape(1, 256))
        pairs = [(0, 0), (0, 1), (1, 0), (1, 1), (0, 2), (2, 0)]
        row16 = lax.broadcasted_iota(jnp.int32, (16, 512), 0)
        left_rows = jnp.zeros((16, 512), jnp.float32)
        right_rows = jnp.zeros((16, 256), jnp.float32)
        for r, (a, b) in enumerate(pairs):
            left_rows = jnp.where(row16 == r, i_parts[a].astype(jnp.float32), left_rows)
            right_rows = jnp.where(row16[:, :256] == r, g_parts[b].astype(jnp.float32), right_rows)
        right_rows = right_rows.astype(jnp.bfloat16)
        for k in range(4):
            rows = slice(k * SPAN, (k + 1) * SPAN)
            factor = dot(left_rows[:, rows].T.astype(jnp.bfloat16), right_rows)
            mamba_ref[rows, :] = (gated[rows, :] * factor).astype(jnp.bfloat16)

    def ring(s, carry):
        for c in range(CHUNKS):

            @pl.when(came_up(s, c))
            def _():
                up_arrival(s, c).wait_recv()

                @pl.when(jnp.logical_and(z < last, s < up_hops(c)))
                def _():
                    up_copy(s, c).start()

                sib_copy(up_block(s), core * 4 + c, sib_send, sib_recv, s * CHUNKS + c).start()

            @pl.when(travels_down(s, c))
            def _():
                down_arrival(s, c).wait_recv()

                @pl.when(s < down_hops(c))
                def _():
                    down_copy(s, c).start()

                @pl.when(z + s >= n_ctx)
                def _():
                    sib_copy(
                        down_block(s), core * 4 + c, sibd_send, sibd_recv, s * CHUNKS + c
                    ).start()

            if c == 0:
                sib_wait(s - 1)
            attend_two(s - 1, c)

        @pl.when(s == STATE_STEP)
        def _():
            send_states()

        @pl.when(s == M4_STEP)
        def _():
            prefix()

        @pl.when(s == M5_STEP)
        def _():
            finish_mixed()

        return carry

    def sib_wait(s):
        for c in range(CHUNKS):

            @pl.when(jnp.logical_and(s >= 1, came_up(s, c)))
            def _():
                sib_copy(
                    up_block(s), (1 - core) * 4 + c, sib_send, sib_recv, s * CHUNKS + c
                ).wait_recv()

            @pl.when(jnp.logical_and(s >= 1, down_useful(s, c)))
            def _():
                sib_copy(
                    down_block(s), (1 - core) * 4 + c, sibd_send, sibd_recv, s * CHUNKS + c
                ).wait_recv()

    def attend_two(s, c):
        up = jnp.logical_and(s >= 1, z >= s)
        down = jnp.logical_and(s >= 1, down_useful(s, 0))

        @pl.when(jnp.logical_and(up, down))
        def _():
            attend((up_block(s), down_block(s)), c)

        @pl.when(jnp.logical_and(up, jnp.logical_not(down)))
        def _():
            attend((up_block(s),), c)

    pl.semaphore_wait(far_sem.at[0], 2)
    tell(1)
    lax.fori_loop(1, UP + 1, ring, 0)
    finish_norm()
    sib_wait(UP)

    @pl.when(z >= UP)
    def _():
        for t in range(4):
            attend((up_block(UP),), t)

    for h in range(2):
        for i in range(4):
            lanes = slice(h * 512 + i * 128, h * 512 + (i + 1) * 128)
            result = acc[:, lanes] / l_run[:, lanes]
            attn_ref[i * 128 : (i + 1) * 128, h * 128 : (h + 1) * 128] = result.T.astype(
                jnp.bfloat16
            )

    def sent(s, carry):
        for c in range(CHUNKS):

            @pl.when(jnp.logical_and(z < last, jnp.logical_and(z >= s, s < up_hops(c))))
            def _():
                up_copy(s, c).wait_send()

            @pl.when(jnp.logical_and(s < down_hops(c), travels_down(s, c)))
            def _():
                down_copy(s, c).wait_send()

        return carry

    def sent_sib(s, carry):
        for c in range(CHUNKS):

            @pl.when(came_up(s, c))
            def _():
                sib_copy(up_block(s), core * 4 + c, sib_send, sib_recv, s * CHUNKS + c).wait_send()

            @pl.when(down_useful(s, c))
            def _():
                sib_copy(
                    down_block(s), core * 4 + c, sibd_send, sibd_recv, s * CHUNKS + c
                ).wait_send()

        return carry

    lax.fori_loop(0, UP, sent, 0)
    lax.fori_loop(1, UP + 1, sent_sib, 0)

    @pl.when(z < last)
    def _():
        each(1, n_ctx, lambda d: (total_copy(d).wait_send(), state_copy(d).wait_send()))

    each(1, n_ctx, lambda d: entering_copy(d).wait_send(), lambda d: other_of(d) > 0)
    for d in range(1, 4):
        square_copy(d).wait_send()


def body(
    n_ctx,
    mixer_input,
    gate_input,
    step_raw,
    decay_log,
    skip_weight,
    state_maps,
    norm_gain,
    queries,
    keys_values,
):
    vmem = pl.BlockSpec(memory_space=pltpu.VMEM)
    smem = pl.BlockSpec(memory_space=pltpu.SMEM)
    hbm = pl.BlockSpec(memory_space=pltpu.HBM)
    dma = pltpu.SemaphoreType.DMA
    rows = mixer_input.shape[0]
    return pl.pallas_call(
        functools.partial(kernel, n_ctx),
        out_shape=(
            pltpu.VMEM((rows, 256), jnp.bfloat16),
            pltpu.VMEM((rows, 256), jnp.bfloat16),
        ),
        in_specs=[smem, smem, vmem, vmem] + [hbm] * 5,
        out_specs=(vmem, vmem),
        scratch_shapes=[
            pltpu.VMEM((rows, 256), jnp.bfloat16),
            pltpu.VMEM((rows, 256), jnp.bfloat16),
            pltpu.VMEM((rows, 256), jnp.bfloat16),
            pltpu.VMEM((rows * 16, 128), jnp.bfloat16),
            pltpu.VMEM((rows * 16, 128), jnp.bfloat16),
            pltpu.VMEM((rows * 16, 128), jnp.float32),
            pltpu.VMEM((2, rows, 128), jnp.bfloat16),
            dma((7,)),
            pltpu.SemaphoreType.REGULAR((2,)),
            pltpu.VMEM((n_ctx, 8, 128, 128), jnp.bfloat16),
            pltpu.VMEM((128, 1024), jnp.bfloat16),
            pltpu.VMEM((1, 1024), jnp.float32),
            pltpu.VMEM((1, 1024), jnp.float32),
            pltpu.VMEM((128, 1024), jnp.float32),
            pltpu.VMEM((512, 256), jnp.float32),
            pltpu.VMEM((512, 256), jnp.float32),
            pltpu.VMEM((512, 256), jnp.float32),
            pltpu.VMEM((n_ctx, 2, 128), jnp.float32),
            pltpu.VMEM((n_ctx, 16, 128), jnp.bfloat16),
            pltpu.VMEM((n_ctx, 16, 128), jnp.bfloat16),
            pltpu.VMEM((n_ctx, 16, 128), jnp.bfloat16),
            pltpu.VMEM((n_ctx, 16, 128), jnp.bfloat16),
            pltpu.VMEM((4, 8, 512), jnp.float32),
            dma((UP * CHUNKS,)),
            dma((UP * CHUNKS,)),
            dma((UP * CHUNKS,)),
            dma((UP * CHUNKS,)),
            dma(((UP + 1) * CHUNKS,)),
            dma(((UP + 1) * CHUNKS,)),
            dma(((UP + 1) * CHUNKS,)),
            dma(((UP + 1) * CHUNKS,)),
            dma((n_ctx,)),
            dma((n_ctx,)),
            dma((n_ctx,)),
            dma((n_ctx,)),
            dma((n_ctx,)),
            dma((n_ctx,)),
            dma((4,)),
            dma((4,)),
        ],
        compiler_params=pltpu.CompilerParams(
            collective_id=0, has_side_effects=True, vmem_limit_bytes=56 * 2**20
        ),
    )(
        decay_log,
        skip_weight,
        step_raw.T,
        norm_gain,
        mixer_input,
        gate_input,
        state_maps.reshape(rows * 16, 128),
        queries,
        keys_values.reshape(rows * 16, 128),
    )


def solution(mesh):
    in_specs = (
        P("ctx", "head"),
        P("ctx", "head"),
        P("ctx", "head"),
        P("head"),
        P("head"),
        P("ctx", None, None, None),
        P("head"),
        P("ctx", "head"),
        P("ctx", None, None, None),
    )
    return jax.shard_map(
        functools.partial(body, mesh.shape["ctx"]),
        mesh=mesh,
        in_specs=in_specs,
        out_specs=(P("ctx", "head"), P("ctx", "head")),
        check_vma=False,
    )
```

```python
import functools
import math

import jax
import jax.numpy as jnp
from jax import lax
from jax.experimental import pallas as pl
from jax.experimental.pallas import tpu as pltpu
from jax.sharding import PartitionSpec as P

MESH = pl.DeviceIdType.MESH
HIGH = lax.Precision.HIGHEST
NEG_FILL = -1e30
EPSILON = 1e-5
SPAN = 128
CHUNKS = 3
UP = 8
DOWN_PIECE = 1
NEAR = 2
EARLY_BLOCKS = {(1, 0): (), (1, 1): (), (1, 2): (0, 1), (2, 0): (), (2, 1): (2,), (2, 2): (3,)}
TILES = ((0, 1), (), (2, 3))
PREFIX_AT = (4, 2)


def softplus(v):
    u = jnp.exp(-jnp.abs(v))
    small = u * (1.0 - u * (0.5 - u * (1.0 / 3.0 - u * 0.25)))
    return jnp.maximum(v, 0.0) + jnp.where(u < 0.02, small, jnp.log(1.0 + u))


def silu(v):
    return v / (1.0 + jnp.exp(-v))


def dot(a, b, **kw):
    return jnp.dot(a, b, preferred_element_type=jnp.float32, **kw)


def parts_of(v):
    high = v.astype(jnp.bfloat16)
    rest = v - high.astype(jnp.float32)
    middle = rest.astype(jnp.bfloat16)
    low = (rest - middle.astype(jnp.float32)).astype(jnp.bfloat16)
    return high, middle, low


def dot_t(a, b, **kw):
    return lax.dot_general(
        a, b, (((1,), (1,)), ((), ())), preferred_element_type=jnp.float32, **kw
    )


def kernel(
    n_ctx,
    decay_ref,
    skip_ref,
    step_ref,
    gain_ref,
    x_hbm,
    gate_hbm,
    maps_hbm,
    q_hbm,
    kv_hbm,
    mamba_ref,
    attn_ref,
    x_ref,
    gate_ref,
    q_ref,
    maps_raw,
    kv_raw,
    wide,
    maps_ref,
    in_sem,
    far_sem,
    kvbuf,
    qt,
    m_run,
    l_run,
    acc,
    mixed,
    decay_t,
    total_buf,
    sbuf,
    srecv,
    ebuf,
    erecv,
    sq_buf,
    up_send,
    up_recv,
    dn_send,
    dn_recv,
    sib_send,
    sib_recv,
    sibd_send,
    sibd_recv,
    y_send,
    y_recv,
    yd_send,
    yd_recv,
    d_send,
    d_recv,
    s_send,
    s_recv,
    e_send,
    e_recv,
    q_send,
    q_recv,
):
    z = lax.axis_index("ctx")
    hd = lax.axis_index("head")
    core = lax.rem(hd, 2)
    sib = hd + 1 - 2 * core
    base = hd - lax.rem(hd, 4)
    place = lax.rem(hd, 4)
    side = place // 2
    across = base + lax.rem(place + 2, 4)
    missing = core * 4 + 3 - 3 * side

    def part(c):
        return core * 4 + c + side * (3 - 2 * c)

    above = lax.rem(z + 1, n_ctx)
    below = lax.rem(z + n_ctx - 1, n_ctx)

    barrier = pltpu.get_barrier_semaphore()
    for d in range(NEAR, 0, -1):
        for other in (lax.rem(z + d, n_ctx), lax.rem(z + n_ctx - d, n_ctx)):
            pl.semaphore_signal(barrier, inc=1, device_id=(other, hd), device_id_type=MESH)
    for d in range(1, 4):
        pl.semaphore_signal(
            barrier, inc=1, device_id=(z, base + lax.rem(place + d, 4)), device_id_type=MESH
        )

    fetches = []
    for src, dst in ((kv_hbm, kv_raw), (maps_hbm, maps_raw)):
        for rows in (pl.ds(0, 4096), pl.ds(4096, 4096)):
            fetches.append((src.at[rows], dst.at[rows]))
    fetches += [(q_hbm, q_ref), (x_hbm, x_ref), (gate_hbm, gate_ref)]
    fetches = [
        pltpu.make_async_copy(src, dst, in_sem.at[i]) for i, (src, dst) in enumerate(fetches)
    ]
    for fetch in fetches:
        fetch.start()

    def pick_group(raw, waits):
        for i, fetch in enumerate(waits):
            fetch.wait()

            def widen(k, carry):
                rows = pl.ds(pl.multiple_of(i * 4096 + k * 512, 512), 512)
                wide[rows, :] = raw[rows, :].astype(jnp.float32)
                return carry

            lax.fori_loop(0, 8, widen, 0)
        return [wide[pl.ds(8 * i + hd // 4, 512, stride=16), :] for i in range(2)]

    keys, values = pick_group(kv_raw, fetches[0:2])
    for i in range(4):
        kvbuf[z, i] = keys[i * 128 : (i + 1) * 128, :].astype(jnp.bfloat16)
        kvbuf[z, 4 + i] = values[i * 128 : (i + 1) * 128, :].T.astype(jnp.bfloat16)

    def up_copy(s, c):
        block = lax.rem(z - s + n_ctx, n_ctx)
        return pltpu.make_async_remote_copy(
            src_ref=kvbuf.at[block, part(c)],
            dst_ref=kvbuf.at[block, part(c)],
            send_sem=up_send.at[s * CHUNKS + c],
            recv_sem=up_recv.at[s * CHUNKS + c],
            device_id=(above, hd),
            device_id_type=MESH,
        )

    def down_copy(s, c):
        block = lax.rem(z + s, n_ctx)
        return pltpu.make_async_remote_copy(
            src_ref=kvbuf.at[block, part(c)],
            dst_ref=kvbuf.at[block, part(c)],
            send_sem=dn_send.at[s * CHUNKS + c],
            recv_sem=dn_recv.at[s * CHUNKS + c],
            device_id=(below, hd),
            device_id_type=MESH,
        )

    def up_arrival(s, c):
        block = lax.rem(z - s + n_ctx, n_ctx)
        return pltpu.make_async_remote_copy(
            src_ref=kvbuf.at[block, part(c)],
            dst_ref=kvbuf.at[block, part(c)],
            send_sem=up_send.at[(s - 1) * CHUNKS + c],
            recv_sem=up_recv.at[(s - 1) * CHUNKS + c],
            device_id=(above, hd),
            device_id_type=MESH,
        )

    def down_arrival(s, c):
        block = lax.rem(z + s, n_ctx)
        return pltpu.make_async_remote_copy(
            src_ref=kvbuf.at[block, part(c)],
            dst_ref=kvbuf.at[block, part(c)],
            send_sem=dn_send.at[(s - 1) * CHUNKS + c],
            recv_sem=dn_recv.at[(s - 1) * CHUNKS + c],
            device_id=(below, hd),
            device_id_type=MESH,
        )

    def sib_copy(block, index, send, recv, i):
        return pltpu.make_async_remote_copy(
            src_ref=kvbuf.at[block, index],
            dst_ref=kvbuf.at[block, index],
            send_sem=send.at[i],
            recv_sem=recv.at[i],
            device_id=(z, sib),
            device_id_type=MESH,
        )

    def y_copy(block, index, send, recv, i):
        return pltpu.make_async_remote_copy(
            src_ref=kvbuf.at[block, index],
            dst_ref=kvbuf.at[block, index],
            send_sem=send.at[i],
            recv_sem=recv.at[i],
            device_id=(z, across),
            device_id_type=MESH,
        )

    def up_block(s):
        return lax.rem(z - s + n_ctx, n_ctx)

    def down_block(s):
        return lax.rem(z + s, n_ctx)

    def up_hops(c):
        return UP - 1 if c == DOWN_PIECE else UP

    def down_hops(c):
        return UP if c == DOWN_PIECE else UP - 1

    def came_up(s, c):
        return jnp.logical_and(z >= s, s <= up_hops(c))

    def travels_down(s, c):
        block = lax.rem(z + s, n_ctx)
        return jnp.logical_and(block < down_hops(c), s <= down_hops(c))

    def down_useful(s, c):
        return jnp.logical_and(z + s >= n_ctx, travels_down(s, c))

    def total_copy(d):
        return pltpu.make_async_remote_copy(
            src_ref=total_buf.at[z],
            dst_ref=total_buf.at[z],
            send_sem=d_send.at[d],
            recv_sem=d_recv.at[z],
            device_id=(lax.rem(z + d, n_ctx), hd),
            device_id_type=MESH,
        )

    def total_arrival(d):
        other = lax.rem(z + d, n_ctx)
        return pltpu.make_async_remote_copy(
            src_ref=total_buf.at[other],
            dst_ref=total_buf.at[other],
            send_sem=d_send.at[d],
            recv_sem=d_recv.at[other],
            device_id=(other, hd),
            device_id_type=MESH,
        )

    def state_copy(d):
        other = lax.rem(z + d, n_ctx)
        return pltpu.make_async_remote_copy(
            src_ref=sbuf.at[other],
            dst_ref=srecv.at[z],
            send_sem=s_send.at[d],
            recv_sem=s_recv.at[z],
            device_id=(other, hd),
            device_id_type=MESH,
        )

    def state_arrival(d):
        other = lax.rem(z + d, n_ctx)
        return pltpu.make_async_remote_copy(
            src_ref=sbuf.at[other],
            dst_ref=srecv.at[other],
            send_sem=s_send.at[d],
            recv_sem=s_recv.at[other],
            device_id=(other, hd),
            device_id_type=MESH,
        )

    def entering_copy(d):
        other = lax.rem(z + d, n_ctx)
        return pltpu.make_async_remote_copy(
            src_ref=ebuf.at[other],
            dst_ref=erecv.at[z],
            send_sem=e_send.at[d],
            recv_sem=e_recv.at[z],
            device_id=(other, hd),
            device_id_type=MESH,
        )

    def entering_arrival(d):
        other = lax.rem(z + d, n_ctx)
        return pltpu.make_async_remote_copy(
            src_ref=ebuf.at[other],
            dst_ref=erecv.at[other],
            send_sem=e_send.at[d],
            recv_sem=e_recv.at[other],
            device_id=(other, hd),
            device_id_type=MESH,
        )

    def each(first, last, action, cond=None):
        def turn(d, carry):
            if cond is None:
                action(d)
            else:

                @pl.when(cond(d))
                def _():
                    action(d)

            return carry

        lax.fori_loop(first, last, turn, 0)

    def other_of(d):
        return lax.rem(z + d, n_ctx)

    last = n_ctx - 1

    pl.semaphore_wait(barrier, 2 * NEAR + 3)
    for c in range(CHUNKS):

        @pl.when(z < n_ctx - 1)
        def _():
            up_copy(0, c).start()

        @pl.when(travels_down(0, c))
        def _():
            down_copy(0, c).start()

    def tell(i):
        d = NEAR * 2**i
        for other in (lax.rem(z + d, n_ctx), lax.rem(z + n_ctx - d, n_ctx)):
            pl.semaphore_signal(far_sem.at[i], inc=1, device_id=(other, hd), device_id_type=MESH)

    tell(0)

    step = step_ref[...]
    raw = jnp.concatenate([step[:, k * SPAN : (k + 1) * SPAN] for k in range(4)], axis=0)
    row16 = lax.broadcasted_iota(jnp.int32, (16, SPAN), 0)
    rate = jnp.zeros((16, SPAN), jnp.float32)
    for h in range(4):
        rate = jnp.where(lax.rem(row16, 4) == h, decay_ref[h], rate)
    dt = softplus(raw)
    ell = -jnp.exp(rate) * dt
    upper = (
        lax.broadcasted_iota(jnp.int32, (SPAN, SPAN), 0)
        <= lax.broadcasted_iota(jnp.int32, (SPAN, SPAN), 1)
    ).astype(jnp.float32)
    cumul = dot(ell, upper, precision=HIGH)
    ends = cumul[:, SPAN - 1 : SPAN]
    tail = jnp.exp(ends - cumul) * dt
    offsets = [jnp.zeros((4, 1), jnp.float32)]
    for k in range(4):
        offsets.append(offsets[-1] + ends[k * 4 : (k + 1) * 4])
    from_start = cumul + jnp.concatenate(offsets[:4], axis=0)
    lane2 = lax.broadcasted_iota(jnp.int32, (2, 128), 1)
    total_rows = []
    for i in range(2):
        a = jnp.broadcast_to(offsets[4][2 * i : 2 * i + 1], (1, 128))
        b = jnp.broadcast_to(offsets[4][2 * i + 1 : 2 * i + 2], (1, 128))
        total_rows.append(jnp.where(lane2[0:1] < 64, a, b))
    total_buf[z] = jnp.concatenate(total_rows, axis=0)

    b_all, c_all = pick_group(maps_raw, fetches[2:4])
    maps_ref[0] = b_all.astype(jnp.bfloat16)
    maps_ref[1] = c_all.astype(jnp.bfloat16)
    fetches[5].wait()
    row_r = lax.broadcasted_iota(jnp.int32, (16, 256), 0)
    head_l = lax.broadcasted_iota(jnp.int32, (16, 256), 1) // 64
    tail_t, start_t = (jnp.concatenate(parts_of(v.T), axis=1) for v in (tail, from_start))
    cumul_t = cumul.T
    cumul_3 = jnp.concatenate(parts_of(cumul_t), axis=1)
    running = None
    run_list = []
    for k in range(4):
        rows = slice(k * SPAN, (k + 1) * SPAN)
        pick = (row_r == k * 4 + head_l).astype(jnp.float32)
        pick_3 = jnp.concatenate([pick.astype(jnp.bfloat16)] * 3, axis=0)
        tail_x = dot(tail_t, pick_3)
        decay_t[rows, :] = jnp.exp(dot(start_t, pick_3))
        loads = (x_ref[rows, :].astype(jnp.float32) * tail_x).astype(jnp.bfloat16)
        fresh = dot(maps_ref[0, rows, :].T, loads)
        end_lane = jnp.sum(jnp.broadcast_to(ends, (16, 256)) * pick, axis=0, keepdims=True)
        running = fresh if k == 0 else jnp.exp(end_lane) * running + fresh
        run_list.append(running)
    for i in range(n_ctx):
        half, r = i // 8, i % 8
        sbuf[i] = running[r * 16 : (r + 1) * 16, half * 128 : (half + 1) * 128].astype(
            jnp.bfloat16
        )

    fetches[4].wait()
    for h in range(2):
        for i in range(4):
            qt[:, h * 512 + i * 128 : h * 512 + (i + 1) * 128] = q_ref[
                i * 128 : (i + 1) * 128, h * 128 : (h + 1) * 128
            ].T

    def send_states():
        pl.semaphore_wait(far_sem.at[1], 2)

        @pl.when(z < last)
        def _():
            each(1, n_ctx, lambda d: (total_copy(d).start(), state_copy(d).start()))

    lane_w = lax.broadcasted_iota(jnp.int32, (SPAN, SPAN), 1)
    below_diag = lax.broadcasted_iota(jnp.int32, (SPAN, SPAN), 0) >= lane_w
    lane_p = lax.broadcasted_iota(jnp.int32, (1, 256), 1) // 64
    skip = jnp.zeros((1, 256), jnp.float32)
    for h in range(4):
        skip = jnp.where(lane_p == h, skip_ref[h], skip)
    left = lane_w < 64
    def inside_block(k):
        rows = slice(k * SPAN, (k + 1) * SPAN)
        b_mat, c_mat = maps_ref[0, rows, :], maps_ref[1, rows, :]
        scores = dot_t(c_mat, b_mat)
        gate = silu(gate_ref[rows, :].astype(jnp.float32))
        decay_t[rows, :] = decay_t[rows, :] * gate
        for pair in range(2):
            lanes = slice(pair * 128, (pair + 1) * 128)
            x_pair = x_ref[rows, lanes]
            weights = []
            for h in (2 * pair, 2 * pair + 1):
                r = k * 4 + h
                spread = cumul_t[:, r : r + 1] - cumul[r : r + 1, :]
                grown = jnp.exp(jnp.where(below_diag, spread, NEG_FILL))
                weights.append((scores * grown * dt[r : r + 1, :]).astype(jnp.bfloat16))
            zero = jnp.zeros_like(x_pair)
            x_two = jnp.concatenate(
                [jnp.where(left, x_pair, zero), jnp.where(left, zero, x_pair)], axis=0
            )
            inside = dot(jnp.concatenate(weights, axis=1), x_two)
            total = inside + skip[:, lanes] * x_pair.astype(jnp.float32)
            mixed[rows, lanes] = total * gate[:, lanes]
        if k > 0:
            pick = (row_r == k * 4 + head_l).astype(jnp.bfloat16)
            grown_in = jnp.exp(dot(cumul_3, jnp.concatenate([pick] * 3, axis=0)))
            mixed[rows, :] += dot(c_mat, run_list[k - 1].astype(jnp.bfloat16)) * (grown_in * gate)

    coef = math.log2(math.e) / math.sqrt(128.0)

    def diagonal(tiles):
        def scores_of(t):
            count = (t % 4 + 1) * 128
            s = dot(kvbuf[z, 0 : t % 4 + 1].reshape(count, 128), qt[:, t * 128 : (t + 1) * 128])
            key = lax.broadcasted_iota(jnp.int32, (count, 128), 0)
            query = lax.broadcasted_iota(jnp.int32, (count, 128), 1) + t % 4 * 128
            return jnp.where(key <= query, s, NEG_FILL)

        following = scores_of(tiles[0])
        for n, t in enumerate(tiles):
            lanes = slice(t * 128, (t + 1) * 128)
            s = following
            if n + 1 < len(tiles):
                following = scores_of(tiles[n + 1])
            m = jnp.max(s, axis=0, keepdims=True)
            p = jnp.exp2((s - m) * coef)
            m_run[:, lanes] = m
            l_run[:, lanes] = jnp.sum(p, axis=0, keepdims=True)
            v_mat = jnp.concatenate([kvbuf[z, 4 + i] for i in range(t % 4 + 1)], axis=1)
            acc[:, lanes] = dot(v_mat, p.astype(jnp.bfloat16))

    ones = jnp.ones((16, 256), jnp.bfloat16)

    def attend(blocks, tiles):
        parts = [(b, i) for b in blocks for i in range(2)]
        lanes_of = [slice(t * 256, (t + 1) * 256) for t in tiles]

        def scores_of(lanes):
            queries = qt[:, lanes]
            return [dot(kvbuf[b, 2 * i : 2 * i + 2].reshape(256, 128), queries) for b, i in parts]

        following = scores_of(lanes_of[0])
        for n, lanes in enumerate(lanes_of):
            scores = following
            if n + 1 < len(lanes_of):
                following = scores_of(lanes_of[n + 1])
            before = m_run[:, lanes]
            m = before
            for s in scores:
                m = jnp.maximum(m, jnp.max(s, axis=0, keepdims=True))
            scale = jnp.exp2((before - m) * coef)
            m_run[:, lanes] = m
            summed = None
            for (b, i), s in zip(parts, scores):
                p = jnp.exp2((s - m) * coef).astype(jnp.bfloat16)
                v_mat = jnp.concatenate([kvbuf[b, 4 + 2 * i], kvbuf[b, 5 + 2 * i]], axis=1)
                part = dot(jnp.concatenate([v_mat, ones], axis=0), p)
                summed = part if summed is None else summed + part
            l_run[:, lanes] = l_run[:, lanes] * scale + summed[128:129]
            acc[:, lanes] = acc[:, lanes] * scale + summed[0:128]

    def prefix():
        each(
            1,
            n_ctx,
            lambda d: (total_arrival(d).wait_recv(), state_arrival(d).wait_recv()),
            lambda d: other_of(d) < last,
        )
        srecv[z] = sbuf[z]
        half = z // 8
        entering = jnp.zeros((16, 128), jnp.float32)
        for k in range(n_ctx):
            ebuf[k] = entering.astype(jnp.bfloat16)
            if k < last:
                entering = (
                    jnp.exp(total_buf[k, pl.ds(half, 1), :]) * entering
                    + srecv[k].astype(jnp.float32)
                )
        erecv[z] = ebuf[z]
        each(1, n_ctx, lambda d: entering_copy(d).start(), lambda d: other_of(d) > 0)

    def finish_mixed():
        @pl.when(z > 0)
        def _():
            each(1, n_ctx, lambda d: entering_arrival(d).wait_recv())
            e_mat = jnp.concatenate(
                [erecv[i * 8 : (i + 1) * 8].reshape(128, 128) for i in range(2)], axis=1
            )
            for k in range(4):
                rows = slice(k * SPAN, (k + 1) * SPAN)
                mixed[rows, :] += dot(maps_ref[1, rows, :], e_mat) * decay_t[rows, :]

        ones8 = jnp.ones((8, 256), jnp.bfloat16)
        for k in range(4):
            rows = slice(k * SPAN, (k + 1) * SPAN)
            value = mixed[rows, :]
            squares = (value * value).astype(jnp.bfloat16)
            sq_buf[place, :, rows] = dot_t(ones8, squares)
        for d in range(1, 4):
            square_copy(d).start()

    def square_copy(d):
        return pltpu.make_async_remote_copy(
            src_ref=sq_buf.at[place],
            dst_ref=sq_buf.at[place],
            send_sem=q_send.at[d],
            recv_sem=q_recv.at[place],
            device_id=(z, base + lax.rem(place + d, 4)),
            device_id_type=MESH,
        )

    def square_arrival(d):
        other = lax.rem(place + d, 4)
        return pltpu.make_async_remote_copy(
            src_ref=sq_buf.at[other],
            dst_ref=sq_buf.at[other],
            send_sem=q_send.at[d],
            recv_sem=q_recv.at[other],
            device_id=(z, base + other),
            device_id_type=MESH,
        )

    def finish_norm():
        for d in range(1, 4):
            square_arrival(d).wait_recv()
        total = sq_buf[0] + sq_buf[1] + sq_buf[2] + sq_buf[3]
        inv = lax.rsqrt(total * (1.0 / 1024.0) + EPSILON)
        i_parts = [v[0:1] for v in parts_of(inv)]
        g_parts = parts_of(gain_ref[...].reshape(1, 256))
        pairs = [(0, 0), (0, 1), (1, 0), (1, 1), (0, 2), (2, 0)]
        row16 = lax.broadcasted_iota(jnp.int32, (16, 512), 0)
        left_rows = jnp.zeros((16, 512), jnp.float32)
        right_rows = jnp.zeros((16, 256), jnp.float32)
        for r, (a, b) in enumerate(pairs):
            left_rows = jnp.where(row16 == r, i_parts[a].astype(jnp.float32), left_rows)
            right_rows = jnp.where(row16[:, :256] == r, g_parts[b].astype(jnp.float32), right_rows)
        right_rows = right_rows.astype(jnp.bfloat16)
        for k in range(4):
            rows = slice(k * SPAN, (k + 1) * SPAN)
            factor = dot(left_rows[:, rows].T.astype(jnp.bfloat16), right_rows)
            mamba_ref[rows, :] = (mixed[rows, :] * factor).astype(jnp.bfloat16)

    def ring(s, carry, early=False):
        for c in range(CHUNKS):

            @pl.when(came_up(s, c))
            def _():
                up_arrival(s, c).wait_recv()

                @pl.when(jnp.logical_and(z < last, s < up_hops(c)))
                def _():
                    up_copy(s, c).start()

            @pl.when(travels_down(s, c))
            def _():
                down_arrival(s, c).wait_recv()

                @pl.when(s < down_hops(c))
                def _():
                    down_copy(s, c).start()

            @pl.when(came_up(s, c))
            def _():
                if c == 0:
                    y_copy(up_block(s), part(c), y_send, y_recv, s).start()
                sib_copy(up_block(s), part(c), sib_send, sib_recv, s * 4 + c).start()

            @pl.when(down_useful(s, c))
            def _():
                if c == 0:
                    y_copy(down_block(s), part(c), yd_send, yd_recv, s).start()
                sib_copy(down_block(s), part(c), sibd_send, sibd_recv, s * 4 + c).start()

            if early:
                if s == 1:
                    if c == 0:
                        fetches[6].wait()
                    if c < 2:
                        diagonal(range(4 * c, 4 * c + 4))
                for k in EARLY_BLOCKS[s, c]:
                    inside_block(k)
                if s == 2 and c == 0:
                    send_states()
                if s == 2 and c == 1:
                    y_wait(1)
                continue
            if c == 0:
                sib_wait(s - 2)
            if c == 1:
                y_wait(s - 1)
            if TILES[c]:
                attend_two(s - 2, TILES[c])
            if c == PREFIX_AT[1]:
                pl.when(s == PREFIX_AT[0])(prefix)
                pl.when(s == 7)(finish_mixed)

        return carry

    def y_wait(s):
        @pl.when(jnp.logical_and(s >= 1, came_up(s, 0)))
        def _():
            y_copy(up_block(s), missing, y_send, y_recv, s).wait_recv()
            sib_copy(up_block(s), missing, sib_send, sib_recv, s * 4 + 3).start()

        @pl.when(jnp.logical_and(s >= 1, down_useful(s, 0)))
        def _():
            y_copy(down_block(s), missing, yd_send, yd_recv, s).wait_recv()
            sib_copy(down_block(s), missing, sibd_send, sibd_recv, s * 4 + 3).start()

    def theirs(index):
        return index + 4 - 8 * core

    def sib_wait(s):
        for c in range(4):
            index, like = (missing, 0) if c == 3 else (part(c), c)

            @pl.when(jnp.logical_and(s >= 1, came_up(s, like)))
            def _():
                sib_copy(up_block(s), theirs(index), sib_send, sib_recv, s * 4 + c).wait_recv()

            @pl.when(jnp.logical_and(s >= 1, down_useful(s, like)))
            def _():
                sib_copy(
                    down_block(s), theirs(index), sibd_send, sibd_recv, s * 4 + c
                ).wait_recv()

    def attend_two(s, c):
        up = jnp.logical_and(s >= 1, z >= s)
        down = jnp.logical_and(s >= 1, down_useful(s, 0))

        @pl.when(jnp.logical_and(up, down))
        def _():
            attend((up_block(s), down_block(s)), c)

        @pl.when(jnp.logical_and(up, jnp.logical_not(down)))
        def _():
            attend((up_block(s),), c)

    pl.semaphore_wait(far_sem.at[0], 2)
    tell(1)
    ring(1, 0, early=True)
    ring(2, 0, early=True)
    lax.fori_loop(3, UP + 1, ring, 0)
    sib_wait(UP - 1)
    attend_two(UP - 1, (0, 1))
    y_wait(UP)
    attend_two(UP - 1, (2, 3))
    finish_norm()
    sib_wait(UP)

    @pl.when(z >= UP)
    def _():
        attend((up_block(UP),), (0, 1, 2, 3))

    for h in range(2):
        for i in range(4):
            lanes = slice(h * 512 + i * 128, h * 512 + (i + 1) * 128)
            result = acc[:, lanes] * (1.0 / l_run[:, lanes])
            attn_ref[i * 128 : (i + 1) * 128, h * 128 : (h + 1) * 128] = result.T.astype(
                jnp.bfloat16
            )

    def sent(s, carry):
        for c in range(CHUNKS):

            @pl.when(jnp.logical_and(z < last, jnp.logical_and(z >= s, s < up_hops(c))))
            def _():
                up_copy(s, c).wait_send()

            @pl.when(jnp.logical_and(s < down_hops(c), travels_down(s, c)))
            def _():
                down_copy(s, c).wait_send()

        return carry

    def sent_here(s, carry):
        for c in range(4):
            index, like = (missing, 0) if c == 3 else (part(c), c)

            @pl.when(came_up(s, like))
            def _():
                sib_copy(up_block(s), index, sib_send, sib_recv, s * 4 + c).wait_send()
                if c == 0:
                    y_copy(up_block(s), index, y_send, y_recv, s).wait_send()

            @pl.when(down_useful(s, like))
            def _():
                sib_copy(down_block(s), index, sibd_send, sibd_recv, s * 4 + c).wait_send()
                if c == 0:
                    y_copy(down_block(s), index, yd_send, yd_recv, s).wait_send()

        return carry

    lax.fori_loop(0, UP, sent, 0)
    lax.fori_loop(1, UP + 1, sent_here, 0)

    @pl.when(z < last)
    def _():
        each(1, n_ctx, lambda d: (total_copy(d).wait_send(), state_copy(d).wait_send()))

    each(1, n_ctx, lambda d: entering_copy(d).wait_send(), lambda d: other_of(d) > 0)
    for d in range(1, 4):
        square_copy(d).wait_send()


def body(
    n_ctx,
    mixer_input,
    gate_input,
    step_raw,
    decay_log,
    skip_weight,
    state_maps,
    norm_gain,
    queries,
    keys_values,
):
    vmem = pl.BlockSpec(memory_space=pltpu.VMEM)
    smem = pl.BlockSpec(memory_space=pltpu.SMEM)
    hbm = pl.BlockSpec(memory_space=pltpu.HBM)
    dma = pltpu.SemaphoreType.DMA
    rows = mixer_input.shape[0]
    return pl.pallas_call(
        functools.partial(kernel, n_ctx),
        out_shape=(
            pltpu.VMEM((rows, 256), jnp.bfloat16),
            pltpu.VMEM((rows, 256), jnp.bfloat16),
        ),
        in_specs=[smem, smem, vmem, vmem] + [hbm] * 5,
        out_specs=(vmem, vmem),
        scratch_shapes=[
            pltpu.VMEM((rows, 256), jnp.bfloat16),
            pltpu.VMEM((rows, 256), jnp.bfloat16),
            pltpu.VMEM((rows, 256), jnp.bfloat16),
            pltpu.VMEM((rows * 16, 128), jnp.bfloat16),
            pltpu.VMEM((rows * 16, 128), jnp.bfloat16),
            pltpu.VMEM((rows * 16, 128), jnp.float32),
            pltpu.VMEM((2, rows, 128), jnp.bfloat16),
            dma((7,)),
            pltpu.SemaphoreType.REGULAR((2,)),
            pltpu.VMEM((n_ctx, 8, 128, 128), jnp.bfloat16),
            pltpu.VMEM((128, 1024), jnp.bfloat16),
            pltpu.VMEM((1, 1024), jnp.float32),
            pltpu.VMEM((1, 1024), jnp.float32),
            pltpu.VMEM((128, 1024), jnp.float32),
            pltpu.VMEM((512, 256), jnp.float32),
            pltpu.VMEM((512, 256), jnp.float32),
            pltpu.VMEM((n_ctx, 2, 128), jnp.float32),
            pltpu.VMEM((n_ctx, 16, 128), jnp.bfloat16),
            pltpu.VMEM((n_ctx, 16, 128), jnp.bfloat16),
            pltpu.VMEM((n_ctx, 16, 128), jnp.bfloat16),
            pltpu.VMEM((n_ctx, 16, 128), jnp.bfloat16),
            pltpu.VMEM((4, 8, 512), jnp.float32),
            dma((UP * CHUNKS,)),
            dma((UP * CHUNKS,)),
            dma((UP * CHUNKS,)),
            dma((UP * CHUNKS,)),
            dma(((UP + 1) * 4,)),
            dma(((UP + 1) * 4,)),
            dma(((UP + 1) * 4,)),
            dma(((UP + 1) * 4,)),
            dma((UP + 1,)),
            dma((UP + 1,)),
            dma((UP + 1,)),
            dma((UP + 1,)),
            dma((n_ctx,)),
            dma((n_ctx,)),
            dma((n_ctx,)),
            dma((n_ctx,)),
            dma((n_ctx,)),
            dma((n_ctx,)),
            dma((4,)),
            dma((4,)),
        ],
        compiler_params=pltpu.CompilerParams(
            collective_id=0, has_side_effects=True, vmem_limit_bytes=56 * 2**20
        ),
    )(
        decay_log,
        skip_weight,
        step_raw.T,
        norm_gain,
        mixer_input,
        gate_input,
        state_maps.reshape(rows * 16, 128),
        queries,
        keys_values.reshape(rows * 16, 128),
    )


def solution(mesh):
    in_specs = (
        P("ctx", "head"),
        P("ctx", "head"),
        P("ctx", "head"),
        P("head"),
        P("head"),
        P("ctx", None, None, None),
        P("head"),
        P("ctx", "head"),
        P("ctx", None, None, None),
    )
    return jax.shard_map(
        functools.partial(body, mesh.shape["ctx"]),
        mesh=mesh,
        in_specs=in_specs,
        out_specs=(P("ctx", "head"), P("ctx", "head")),
        check_vma=False,
    )
```

```python
import functools
import math

import jax
import jax.numpy as jnp
from jax import lax
from jax.experimental import pallas as pl
from jax.experimental.pallas import tpu as pltpu
from jax.sharding import PartitionSpec as P

MESH = pl.DeviceIdType.MESH
HIGH = lax.Precision.HIGHEST
NEG_FILL = -1e30
EPSILON = 1e-5
SPAN = 128
CHUNKS = 3
UP = 8
DOWN_PIECE = 1
NEAR = 2
EARLY_BLOCKS = {(1, 0): (), (1, 1): (), (1, 2): (0, 1), (2, 0): (), (2, 1): (2,), (2, 2): (3,)}
TILES = ((0, 1), (), (2, 3))
PREFIX_AT = (4, 2)


def softplus(v):
    u = jnp.exp(-jnp.abs(v))
    small = u * (1.0 - u * (0.5 - u * (1.0 / 3.0 - u * 0.25)))
    return jnp.maximum(v, 0.0) + jnp.where(u < 0.02, small, jnp.log(1.0 + u))


def silu(v):
    return v / (1.0 + jnp.exp(-v))


def dot(a, b, **kw):
    return jnp.dot(a, b, preferred_element_type=jnp.float32, **kw)


def parts_of(v):
    high = v.astype(jnp.bfloat16)
    rest = v - high.astype(jnp.float32)
    middle = rest.astype(jnp.bfloat16)
    low = (rest - middle.astype(jnp.float32)).astype(jnp.bfloat16)
    return high, middle, low


def dot_t(a, b, **kw):
    return lax.dot_general(
        a, b, (((1,), (1,)), ((), ())), preferred_element_type=jnp.float32, **kw
    )


def kernel(
    n_ctx,
    decay_ref,
    skip_ref,
    step_ref,
    gain_ref,
    x_hbm,
    gate_hbm,
    maps_hbm,
    q_hbm,
    kv_hbm,
    mamba_ref,
    attn_ref,
    x_ref,
    gate_ref,
    q_ref,
    maps_raw,
    kv_raw,
    wide,
    maps_ref,
    in_sem,
    far_sem,
    kvbuf,
    qt,
    m_run,
    l_run,
    acc,
    mixed,
    decay_t,
    total_buf,
    sbuf,
    srecv,
    ebuf,
    erecv,
    sq_buf,
    up_send,
    up_recv,
    dn_send,
    dn_recv,
    sib_send,
    sib_recv,
    sibd_send,
    sibd_recv,
    y_send,
    y_recv,
    yd_send,
    yd_recv,
    d_send,
    d_recv,
    s_send,
    s_recv,
    e_send,
    e_recv,
    q_send,
    q_recv,
):
    z = lax.axis_index("ctx")
    hd = lax.axis_index("head")
    core = lax.rem(hd, 2)
    sib = hd + 1 - 2 * core
    base = hd - lax.rem(hd, 4)
    place = lax.rem(hd, 4)
    side = place // 2
    across = base + lax.rem(place + 2, 4)
    missing = core * 4 + 3 - 3 * side

    def part(c):
        return core * 4 + c + side * (3 - 2 * c)

    above = lax.rem(z + 1, n_ctx)
    below = lax.rem(z + n_ctx - 1, n_ctx)

    barrier = pltpu.get_barrier_semaphore()
    for d in range(NEAR, 0, -1):
        for other in (lax.rem(z + d, n_ctx), lax.rem(z + n_ctx - d, n_ctx)):
            pl.semaphore_signal(barrier, inc=1, device_id=(other, hd), device_id_type=MESH)
    for d in range(1, 4):
        pl.semaphore_signal(
            barrier, inc=1, device_id=(z, base + lax.rem(place + d, 4)), device_id_type=MESH
        )

    fetches = []
    for src, dst in ((kv_hbm, kv_raw), (maps_hbm, maps_raw)):
        for rows in (pl.ds(0, 4096), pl.ds(4096, 4096)):
            fetches.append((src.at[rows], dst.at[rows]))
    fetches += [(q_hbm, q_ref), (x_hbm, x_ref), (gate_hbm, gate_ref)]
    fetches = [
        pltpu.make_async_copy(src, dst, in_sem.at[i]) for i, (src, dst) in enumerate(fetches)
    ]
    for fetch in fetches:
        fetch.start()

    def pick_group(raw, waits):
        for i, fetch in enumerate(waits):
            fetch.wait()

            def widen(k, carry):
                rows = pl.ds(pl.multiple_of(i * 4096 + k * 512, 512), 512)
                wide[rows, :] = raw[rows, :].astype(jnp.float32)
                return carry

            lax.fori_loop(0, 8, widen, 0)
        return [wide[pl.ds(8 * i + hd // 4, 512, stride=16), :] for i in range(2)]

    keys, values = pick_group(kv_raw, fetches[0:2])
    for i in range(4):
        kvbuf[z, i] = keys[i * 128 : (i + 1) * 128, :].astype(jnp.bfloat16)
        kvbuf[z, 4 + i] = values[i * 128 : (i + 1) * 128, :].T.astype(jnp.bfloat16)

    def up_copy(s, c):
        block = lax.rem(z - s + n_ctx, n_ctx)
        return pltpu.make_async_remote_copy(
            src_ref=kvbuf.at[block, part(c)],
            dst_ref=kvbuf.at[block, part(c)],
            send_sem=up_send.at[s * CHUNKS + c],
            recv_sem=up_recv.at[s * CHUNKS + c],
            device_id=(above, hd),
            device_id_type=MESH,
        )

    def down_copy(s, c):
        block = lax.rem(z + s, n_ctx)
        return pltpu.make_async_remote_copy(
            src_ref=kvbuf.at[block, part(c)],
            dst_ref=kvbuf.at[block, part(c)],
            send_sem=dn_send.at[s * CHUNKS + c],
            recv_sem=dn_recv.at[s * CHUNKS + c],
            device_id=(below, hd),
            device_id_type=MESH,
        )

    def up_arrival(s, c):
        block = lax.rem(z - s + n_ctx, n_ctx)
        return pltpu.make_async_remote_copy(
            src_ref=kvbuf.at[block, part(c)],
            dst_ref=kvbuf.at[block, part(c)],
            send_sem=up_send.at[(s - 1) * CHUNKS + c],
            recv_sem=up_recv.at[(s - 1) * CHUNKS + c],
            device_id=(above, hd),
            device_id_type=MESH,
        )

    def down_arrival(s, c):
        block = lax.rem(z + s, n_ctx)
        return pltpu.make_async_remote_copy(
            src_ref=kvbuf.at[block, part(c)],
            dst_ref=kvbuf.at[block, part(c)],
            send_sem=dn_send.at[(s - 1) * CHUNKS + c],
            recv_sem=dn_recv.at[(s - 1) * CHUNKS + c],
            device_id=(below, hd),
            device_id_type=MESH,
        )

    def sib_copy(block, index, send, recv, i):
        return pltpu.make_async_remote_copy(
            src_ref=kvbuf.at[block, index],
            dst_ref=kvbuf.at[block, index],
            send_sem=send.at[i],
            recv_sem=recv.at[i],
            device_id=(z, sib),
            device_id_type=MESH,
        )

    def y_copy(block, index, send, recv, i):
        return pltpu.make_async_remote_copy(
            src_ref=kvbuf.at[block, index],
            dst_ref=kvbuf.at[block, index],
            send_sem=send.at[i],
            recv_sem=recv.at[i],
            device_id=(z, across),
            device_id_type=MESH,
        )

    def up_block(s):
        return lax.rem(z - s + n_ctx, n_ctx)

    def down_block(s):
        return lax.rem(z + s, n_ctx)

    def up_hops(c):
        return UP - 1 if c == DOWN_PIECE else UP

    def down_hops(c):
        return UP if c == DOWN_PIECE else UP - 1

    def came_up(s, c):
        return jnp.logical_and(z >= s, s <= up_hops(c))

    def travels_down(s, c):
        block = lax.rem(z + s, n_ctx)
        return jnp.logical_and(block < down_hops(c), s <= down_hops(c))

    def down_useful(s, c):
        return jnp.logical_and(z + s >= n_ctx, travels_down(s, c))

    def total_copy(d):
        return pltpu.make_async_remote_copy(
            src_ref=total_buf.at[z],
            dst_ref=total_buf.at[z],
            send_sem=d_send.at[d],
            recv_sem=d_recv.at[z],
            device_id=(lax.rem(z + d, n_ctx), hd),
            device_id_type=MESH,
        )

    def total_arrival(d):
        other = lax.rem(z + d, n_ctx)
        return pltpu.make_async_remote_copy(
            src_ref=total_buf.at[other],
            dst_ref=total_buf.at[other],
            send_sem=d_send.at[d],
            recv_sem=d_recv.at[other],
            device_id=(other, hd),
            device_id_type=MESH,
        )

    def state_copy(d):
        other = lax.rem(z + d, n_ctx)
        return pltpu.make_async_remote_copy(
            src_ref=sbuf.at[other],
            dst_ref=srecv.at[z],
            send_sem=s_send.at[d],
            recv_sem=s_recv.at[z],
            device_id=(other, hd),
            device_id_type=MESH,
        )

    def state_arrival(d):
        other = lax.rem(z + d, n_ctx)
        return pltpu.make_async_remote_copy(
            src_ref=sbuf.at[other],
            dst_ref=srecv.at[other],
            send_sem=s_send.at[d],
            recv_sem=s_recv.at[other],
            device_id=(other, hd),
            device_id_type=MESH,
        )

    def entering_copy(d):
        other = lax.rem(z + d, n_ctx)
        return pltpu.make_async_remote_copy(
            src_ref=ebuf.at[other],
            dst_ref=erecv.at[z],
            send_sem=e_send.at[d],
            recv_sem=e_recv.at[z],
            device_id=(other, hd),
            device_id_type=MESH,
        )

    def entering_arrival(d):
        other = lax.rem(z + d, n_ctx)
        return pltpu.make_async_remote_copy(
            src_ref=ebuf.at[other],
            dst_ref=erecv.at[other],
            send_sem=e_send.at[d],
            recv_sem=e_recv.at[other],
            device_id=(other, hd),
            device_id_type=MESH,
        )

    def each(first, last, action, cond=None):
        def turn(d, carry):
            if cond is None:
                action(d)
            else:

                @pl.when(cond(d))
                def _():
                    action(d)

            return carry

        lax.fori_loop(first, last, turn, 0)

    def other_of(d):
        return lax.rem(z + d, n_ctx)

    last = n_ctx - 1

    pl.semaphore_wait(barrier, 2 * NEAR + 3)
    for c in range(CHUNKS):

        @pl.when(z < n_ctx - 1)
        def _():
            up_copy(0, c).start()

        @pl.when(travels_down(0, c))
        def _():
            down_copy(0, c).start()

    def tell(i):
        d = NEAR * 2**i
        for other in (lax.rem(z + d, n_ctx), lax.rem(z + n_ctx - d, n_ctx)):
            pl.semaphore_signal(far_sem.at[i], inc=1, device_id=(other, hd), device_id_type=MESH)

    tell(0)

    step = step_ref[...]
    raw = jnp.concatenate([step[:, k * SPAN : (k + 1) * SPAN] for k in range(4)], axis=0)
    row16 = lax.broadcasted_iota(jnp.int32, (16, SPAN), 0)
    rate = jnp.zeros((16, SPAN), jnp.float32)
    for h in range(4):
        rate = jnp.where(lax.rem(row16, 4) == h, decay_ref[h], rate)
    dt = softplus(raw)
    ell = -jnp.exp(rate) * dt
    upper = (
        lax.broadcasted_iota(jnp.int32, (SPAN, SPAN), 0)
        <= lax.broadcasted_iota(jnp.int32, (SPAN, SPAN), 1)
    ).astype(jnp.float32)
    cumul = dot(ell, upper, precision=HIGH)
    ends = cumul[:, SPAN - 1 : SPAN]
    tail = jnp.exp(ends - cumul) * dt
    offsets = [jnp.zeros((4, 1), jnp.float32)]
    for k in range(4):
        offsets.append(offsets[-1] + ends[k * 4 : (k + 1) * 4])
    from_start = cumul + jnp.concatenate(offsets[:4], axis=0)
    lane2 = lax.broadcasted_iota(jnp.int32, (2, 128), 1)
    total_rows = []
    for i in range(2):
        a = jnp.broadcast_to(offsets[4][2 * i : 2 * i + 1], (1, 128))
        b = jnp.broadcast_to(offsets[4][2 * i + 1 : 2 * i + 2], (1, 128))
        total_rows.append(jnp.where(lane2[0:1] < 64, a, b))
    total_buf[z] = jnp.concatenate(total_rows, axis=0)

    b_all, c_all = pick_group(maps_raw, fetches[2:4])
    maps_ref[0] = b_all.astype(jnp.bfloat16)
    maps_ref[1] = c_all.astype(jnp.bfloat16)
    fetches[5].wait()
    row_r = lax.broadcasted_iota(jnp.int32, (16, 256), 0)
    head_l = lax.broadcasted_iota(jnp.int32, (16, 256), 1) // 64
    tail_t, start_t = (jnp.concatenate(parts_of(v.T), axis=1) for v in (tail, from_start))
    cumul_t = cumul.T
    cumul_3 = jnp.concatenate(parts_of(cumul_t), axis=1)
    running = None
    run_list = []
    for k in range(4):
        rows = slice(k * SPAN, (k + 1) * SPAN)
        pick = (row_r == k * 4 + head_l).astype(jnp.float32)
        pick_3 = jnp.concatenate([pick.astype(jnp.bfloat16)] * 3, axis=0)
        tail_x = dot(tail_t, pick_3)
        decay_t[rows, :] = jnp.exp(dot(start_t, pick_3))
        loads = (x_ref[rows, :].astype(jnp.float32) * tail_x).astype(jnp.bfloat16)
        fresh = dot(maps_ref[0, rows, :].T, loads)
        end_lane = jnp.sum(jnp.broadcast_to(ends, (16, 256)) * pick, axis=0, keepdims=True)
        running = fresh if k == 0 else jnp.exp(end_lane) * running + fresh
        run_list.append(running)
    for i in range(n_ctx):
        half, r = i // 8, i % 8
        sbuf[i] = running[r * 16 : (r + 1) * 16, half * 128 : (half + 1) * 128].astype(
            jnp.bfloat16
        )

    fetches[4].wait()
    for h in range(2):
        for i in range(4):
            qt[:, h * 512 + i * 128 : h * 512 + (i + 1) * 128] = q_ref[
                i * 128 : (i + 1) * 128, h * 128 : (h + 1) * 128
            ].T

    def send_states():
        pl.semaphore_wait(far_sem.at[1], 2)

        @pl.when(z < last)
        def _():
            each(1, n_ctx, lambda d: (total_copy(d).start(), state_copy(d).start()))

    lane_w = lax.broadcasted_iota(jnp.int32, (SPAN, SPAN), 1)
    below_diag = lax.broadcasted_iota(jnp.int32, (SPAN, SPAN), 0) >= lane_w
    lane_p = lax.broadcasted_iota(jnp.int32, (1, 256), 1) // 64
    skip = jnp.zeros((1, 256), jnp.float32)
    for h in range(4):
        skip = jnp.where(lane_p == h, skip_ref[h], skip)
    left = lane_w < 64
    def inside_block(k):
        rows = slice(k * SPAN, (k + 1) * SPAN)
        b_mat, c_mat = maps_ref[0, rows, :], maps_ref[1, rows, :]
        scores = dot_t(c_mat, b_mat)
        gate = silu(gate_ref[rows, :].astype(jnp.float32))
        decay_t[rows, :] = decay_t[rows, :] * gate
        for pair in range(2):
            lanes = slice(pair * 128, (pair + 1) * 128)
            x_pair = x_ref[rows, lanes]
            weights = []
            for h in (2 * pair, 2 * pair + 1):
                r = k * 4 + h
                spread = cumul_t[:, r : r + 1] - cumul[r : r + 1, :]
                grown = jnp.exp(jnp.where(below_diag, spread, NEG_FILL))
                weights.append((scores * grown * dt[r : r + 1, :]).astype(jnp.bfloat16))
            zero = jnp.zeros_like(x_pair)
            x_two = jnp.concatenate(
                [jnp.where(left, x_pair, zero), jnp.where(left, zero, x_pair)], axis=0
            )
            inside = dot(jnp.concatenate(weights, axis=1), x_two)
            total = inside + skip[:, lanes] * x_pair.astype(jnp.float32)
            mixed[rows, lanes] = total * gate[:, lanes]
        if k > 0:
            pick = (row_r == k * 4 + head_l).astype(jnp.bfloat16)
            grown_in = jnp.exp(dot(cumul_3, jnp.concatenate([pick] * 3, axis=0)))
            mixed[rows, :] += dot(c_mat, run_list[k - 1].astype(jnp.bfloat16)) * (grown_in * gate)

    coef = math.log2(math.e) / math.sqrt(128.0)

    def diagonal(tiles):
        def scores_of(t):
            count = (t % 4 + 1) * 128
            s = dot(kvbuf[z, 0 : t % 4 + 1].reshape(count, 128), qt[:, t * 128 : (t + 1) * 128])
            key = lax.broadcasted_iota(jnp.int32, (count, 128), 0)
            query = lax.broadcasted_iota(jnp.int32, (count, 128), 1) + t % 4 * 128
            return jnp.where(key <= query, s, NEG_FILL)

        following = scores_of(tiles[0])
        for n, t in enumerate(tiles):
            lanes = slice(t * 128, (t + 1) * 128)
            s = following
            if n + 1 < len(tiles):
                following = scores_of(tiles[n + 1])
            m = jnp.max(s, axis=0, keepdims=True)
            p = jnp.exp2((s - m) * coef)
            m_run[:, lanes] = m
            l_run[:, lanes] = jnp.sum(p, axis=0, keepdims=True)
            v_mat = jnp.concatenate([kvbuf[z, 4 + i] for i in range(t % 4 + 1)], axis=1)
            acc[:, lanes] = dot(v_mat, p.astype(jnp.bfloat16))

    ones = jnp.ones((16, 256), jnp.bfloat16)

    def attend(blocks, tiles):
        parts = [(b, i) for b in blocks for i in range(2)]
        lanes_of = [slice(t * 256, (t + 1) * 256) for t in tiles]

        def scores_of(lanes):
            queries = qt[:, lanes]
            return [dot(kvbuf[b, 2 * i : 2 * i + 2].reshape(256, 128), queries) for b, i in parts]

        following = scores_of(lanes_of[0])
        for n, lanes in enumerate(lanes_of):
            scores = following
            if n + 1 < len(lanes_of):
                following = scores_of(lanes_of[n + 1])
            before = m_run[:, lanes]
            m = before
            for s in scores:
                m = jnp.maximum(m, jnp.max(s, axis=0, keepdims=True))
            scale = jnp.exp2((before - m) * coef)
            m_run[:, lanes] = m
            summed = None
            for (b, i), s in zip(parts, scores):
                p = jnp.exp2((s - m) * coef).astype(jnp.bfloat16)
                v_mat = jnp.concatenate([kvbuf[b, 4 + 2 * i], kvbuf[b, 5 + 2 * i]], axis=1)
                part = dot(jnp.concatenate([v_mat, ones], axis=0), p)
                summed = part if summed is None else summed + part
            l_run[:, lanes] = l_run[:, lanes] * scale + summed[128:129]
            acc[:, lanes] = acc[:, lanes] * scale + summed[0:128]

    def prefix():
        each(
            1,
            n_ctx,
            lambda d: (total_arrival(d).wait_recv(), state_arrival(d).wait_recv()),
            lambda d: other_of(d) < last,
        )
        srecv[z] = sbuf[z]
        half = z // 8
        entering = jnp.zeros((16, 128), jnp.float32)
        for k in range(n_ctx):
            ebuf[k] = entering.astype(jnp.bfloat16)
            if k < last:
                entering = (
                    jnp.exp(total_buf[k, pl.ds(half, 1), :]) * entering
                    + srecv[k].astype(jnp.float32)
                )
        erecv[z] = ebuf[z]
        each(1, n_ctx, lambda d: entering_copy(d).start(), lambda d: other_of(d) > 0)

    def finish_mixed():
        @pl.when(z > 0)
        def _():
            each(1, n_ctx, lambda d: entering_arrival(d).wait_recv())
            e_mat = jnp.concatenate(
                [erecv[i * 8 : (i + 1) * 8].reshape(128, 128) for i in range(2)], axis=1
            )
            for k in range(4):
                rows = slice(k * SPAN, (k + 1) * SPAN)
                mixed[rows, :] += dot(maps_ref[1, rows, :], e_mat) * decay_t[rows, :]

        ones8 = jnp.ones((8, 256), jnp.bfloat16)
        for k in range(4):
            rows = slice(k * SPAN, (k + 1) * SPAN)
            value = mixed[rows, :]
            squares = (value * value).astype(jnp.bfloat16)
            sq_buf[place, :, rows] = dot_t(ones8, squares)
        for d in range(1, 4):
            square_copy(d).start()

    def square_copy(d):
        return pltpu.make_async_remote_copy(
            src_ref=sq_buf.at[place],
            dst_ref=sq_buf.at[place],
            send_sem=q_send.at[d],
            recv_sem=q_recv.at[place],
            device_id=(z, base + lax.rem(place + d, 4)),
            device_id_type=MESH,
        )

    def square_arrival(d):
        other = lax.rem(place + d, 4)
        return pltpu.make_async_remote_copy(
            src_ref=sq_buf.at[other],
            dst_ref=sq_buf.at[other],
            send_sem=q_send.at[d],
            recv_sem=q_recv.at[other],
            device_id=(z, base + other),
            device_id_type=MESH,
        )

    def finish_norm():
        for d in range(1, 4):
            square_arrival(d).wait_recv()
        total = sq_buf[0] + sq_buf[1] + sq_buf[2] + sq_buf[3]
        inv = lax.rsqrt(total * (1.0 / 1024.0) + EPSILON)
        i_parts = [v[0:1] for v in parts_of(inv)]
        g_parts = parts_of(gain_ref[...].reshape(1, 256))
        pairs = [(0, 0), (0, 1), (1, 0), (1, 1), (0, 2), (2, 0)]
        row16 = lax.broadcasted_iota(jnp.int32, (16, 512), 0)
        left_rows = jnp.zeros((16, 512), jnp.float32)
        right_rows = jnp.zeros((16, 256), jnp.float32)
        for r, (a, b) in enumerate(pairs):
            left_rows = jnp.where(row16 == r, i_parts[a].astype(jnp.float32), left_rows)
            right_rows = jnp.where(row16[:, :256] == r, g_parts[b].astype(jnp.float32), right_rows)
        right_rows = right_rows.astype(jnp.bfloat16)
        for k in range(4):
            rows = slice(k * SPAN, (k + 1) * SPAN)
            factor = dot(left_rows[:, rows].T.astype(jnp.bfloat16), right_rows)
            mamba_ref[rows, :] = (mixed[rows, :] * factor).astype(jnp.bfloat16)

    def ring(s, carry, early=False):
        for c in range(CHUNKS):

            @pl.when(came_up(s, c))
            def _():
                up_arrival(s, c).wait_recv()

                @pl.when(jnp.logical_and(z < last, s < up_hops(c)))
                def _():
                    up_copy(s, c).start()

            @pl.when(travels_down(s, c))
            def _():
                down_arrival(s, c).wait_recv()

                @pl.when(s < down_hops(c))
                def _():
                    down_copy(s, c).start()

            @pl.when(came_up(s, c))
            def _():
                if c == 0:
                    y_copy(up_block(s), part(c), y_send, y_recv, s).start()
                sib_copy(up_block(s), part(c), sib_send, sib_recv, s * 4 + c).start()

            @pl.when(down_useful(s, c))
            def _():
                if c == 0:
                    y_copy(down_block(s), part(c), yd_send, yd_recv, s).start()
                sib_copy(down_block(s), part(c), sibd_send, sibd_recv, s * 4 + c).start()

            if early:
                if s == 1:
                    if c == 0:
                        fetches[6].wait()
                    if c < 2:
                        diagonal(range(4 * c, 4 * c + 4))
                for k in EARLY_BLOCKS[s, c]:
                    inside_block(k)
                if s == 2 and c == 2:
                    send_states()
                if s == 2 and c == 1:
                    y_wait(1)
                continue
            if c == 0:
                sib_wait(s - 2)
            if c == 1:
                y_wait(s - 1)
            if TILES[c]:
                attend_two(s - 2, TILES[c])
            if c == PREFIX_AT[1]:
                pl.when(s == PREFIX_AT[0])(prefix)
                pl.when(s == jnp.where(z == 0, 4, 7))(finish_mixed)

        return carry

    def y_wait(s):
        @pl.when(jnp.logical_and(s >= 1, came_up(s, 0)))
        def _():
            y_copy(up_block(s), missing, y_send, y_recv, s).wait_recv()
            sib_copy(up_block(s), missing, sib_send, sib_recv, s * 4 + 3).start()

        @pl.when(jnp.logical_and(s >= 1, down_useful(s, 0)))
        def _():
            y_copy(down_block(s), missing, yd_send, yd_recv, s).wait_recv()
            sib_copy(down_block(s), missing, sibd_send, sibd_recv, s * 4 + 3).start()

    def theirs(index):
        return index + 4 - 8 * core

    def sib_wait(s):
        for c in range(4):
            index, like = (missing, 0) if c == 3 else (part(c), c)

            @pl.when(jnp.logical_and(s >= 1, came_up(s, like)))
            def _():
                sib_copy(up_block(s), theirs(index), sib_send, sib_recv, s * 4 + c).wait_recv()

            @pl.when(jnp.logical_and(s >= 1, down_useful(s, like)))
            def _():
                sib_copy(
                    down_block(s), theirs(index), sibd_send, sibd_recv, s * 4 + c
                ).wait_recv()

    def attend_two(s, c):
        up = jnp.logical_and(s >= 1, z >= s)
        down = jnp.logical_and(s >= 1, down_useful(s, 0))

        @pl.when(jnp.logical_and(up, down))
        def _():
            attend((up_block(s), down_block(s)), c)

        @pl.when(jnp.logical_and(up, jnp.logical_not(down)))
        def _():
            attend((up_block(s),), c)

    pl.semaphore_wait(far_sem.at[0], 2)
    tell(1)
    ring(1, 0, early=True)
    ring(2, 0, early=True)
    lax.fori_loop(3, UP + 1, ring, 0)
    sib_wait(UP - 1)
    attend_two(UP - 1, (0, 1))
    y_wait(UP)
    attend_two(UP - 1, (2, 3))
    finish_norm()
    sib_wait(UP)

    @pl.when(z >= UP)
    def _():
        attend((up_block(UP),), (0, 1, 2, 3))

    for h in range(2):
        for i in range(4):
            lanes = slice(h * 512 + i * 128, h * 512 + (i + 1) * 128)
            result = acc[:, lanes] * (1.0 / l_run[:, lanes])
            attn_ref[i * 128 : (i + 1) * 128, h * 128 : (h + 1) * 128] = result.T.astype(
                jnp.bfloat16
            )

    def sent(s, carry):
        for c in range(CHUNKS):

            @pl.when(jnp.logical_and(z < last, jnp.logical_and(z >= s, s < up_hops(c))))
            def _():
                up_copy(s, c).wait_send()

            @pl.when(jnp.logical_and(s < down_hops(c), travels_down(s, c)))
            def _():
                down_copy(s, c).wait_send()

        return carry

    def sent_here(s, carry):
        for c in range(4):
            index, like = (missing, 0) if c == 3 else (part(c), c)

            @pl.when(came_up(s, like))
            def _():
                sib_copy(up_block(s), index, sib_send, sib_recv, s * 4 + c).wait_send()
                if c == 0:
                    y_copy(up_block(s), index, y_send, y_recv, s).wait_send()

            @pl.when(down_useful(s, like))
            def _():
                sib_copy(down_block(s), index, sibd_send, sibd_recv, s * 4 + c).wait_send()
                if c == 0:
                    y_copy(down_block(s), index, yd_send, yd_recv, s).wait_send()

        return carry

    lax.fori_loop(0, UP, sent, 0)
    lax.fori_loop(1, UP + 1, sent_here, 0)

    @pl.when(z < last)
    def _():
        each(1, n_ctx, lambda d: (total_copy(d).wait_send(), state_copy(d).wait_send()))

    each(1, n_ctx, lambda d: entering_copy(d).wait_send(), lambda d: other_of(d) > 0)
    for d in range(1, 4):
        square_copy(d).wait_send()


def body(
    n_ctx,
    mixer_input,
    gate_input,
    step_raw,
    decay_log,
    skip_weight,
    state_maps,
    norm_gain,
    queries,
    keys_values,
):
    vmem = pl.BlockSpec(memory_space=pltpu.VMEM)
    smem = pl.BlockSpec(memory_space=pltpu.SMEM)
    hbm = pl.BlockSpec(memory_space=pltpu.HBM)
    dma = pltpu.SemaphoreType.DMA
    rows = mixer_input.shape[0]
    return pl.pallas_call(
        functools.partial(kernel, n_ctx),
        out_shape=(
            pltpu.VMEM((rows, 256), jnp.bfloat16),
            pltpu.VMEM((rows, 256), jnp.bfloat16),
        ),
        in_specs=[smem, smem, vmem, vmem] + [hbm] * 5,
        out_specs=(vmem, vmem),
        scratch_shapes=[
            pltpu.VMEM((rows, 256), jnp.bfloat16),
            pltpu.VMEM((rows, 256), jnp.bfloat16),
            pltpu.VMEM((rows, 256), jnp.bfloat16),
            pltpu.VMEM((rows * 16, 128), jnp.bfloat16),
            pltpu.VMEM((rows * 16, 128), jnp.bfloat16),
            pltpu.VMEM((rows * 16, 128), jnp.float32),
            pltpu.VMEM((2, rows, 128), jnp.bfloat16),
            dma((7,)),
            pltpu.SemaphoreType.REGULAR((2,)),
            pltpu.VMEM((n_ctx, 8, 128, 128), jnp.bfloat16),
            pltpu.VMEM((128, 1024), jnp.bfloat16),
            pltpu.VMEM((1, 1024), jnp.float32),
            pltpu.VMEM((1, 1024), jnp.float32),
            pltpu.VMEM((128, 1024), jnp.float32),
            pltpu.VMEM((512, 256), jnp.float32),
            pltpu.VMEM((512, 256), jnp.float32),
            pltpu.VMEM((n_ctx, 2, 128), jnp.float32),
            pltpu.VMEM((n_ctx, 16, 128), jnp.bfloat16),
            pltpu.VMEM((n_ctx, 16, 128), jnp.bfloat16),
            pltpu.VMEM((n_ctx, 16, 128), jnp.bfloat16),
            pltpu.VMEM((n_ctx, 16, 128), jnp.bfloat16),
            pltpu.VMEM((4, 8, 512), jnp.float32),
            dma((UP * CHUNKS,)),
            dma((UP * CHUNKS,)),
            dma((UP * CHUNKS,)),
            dma((UP * CHUNKS,)),
            dma(((UP + 1) * 4,)),
            dma(((UP + 1) * 4,)),
            dma(((UP + 1) * 4,)),
            dma(((UP + 1) * 4,)),
            dma((UP + 1,)),
            dma((UP + 1,)),
            dma((UP + 1,)),
            dma((UP + 1,)),
            dma((n_ctx,)),
            dma((n_ctx,)),
            dma((n_ctx,)),
            dma((n_ctx,)),
            dma((n_ctx,)),
            dma((n_ctx,)),
            dma((4,)),
            dma((4,)),
        ],
        compiler_params=pltpu.CompilerParams(
            collective_id=0, has_side_effects=True, vmem_limit_bytes=56 * 2**20
        ),
    )(
        decay_log,
        skip_weight,
        step_raw.T,
        norm_gain,
        mixer_input,
        gate_input,
        state_maps.reshape(rows * 16, 128),
        queries,
        keys_values.reshape(rows * 16, 128),
    )


def solution(mesh):
    in_specs = (
        P("ctx", "head"),
        P("ctx", "head"),
        P("ctx", "head"),
        P("head"),
        P("head"),
        P("ctx", None, None, None),
        P("head"),
        P("ctx", "head"),
        P("ctx", None, None, None),
    )
    return jax.shard_map(
        functools.partial(body, mesh.shape["ctx"]),
        mesh=mesh,
        in_specs=in_specs,
        out_specs=(P("ctx", "head"), P("ctx", "head")),
        check_vma=False,
    )
```

```python
import functools
import math

import jax
import jax.numpy as jnp
from jax import lax
from jax.experimental import pallas as pl
from jax.experimental.pallas import tpu as pltpu
from jax.sharding import PartitionSpec as P

MESH = pl.DeviceIdType.MESH
HIGH = lax.Precision.HIGHEST
NEG_FILL = -1e30
EPSILON = 1e-5
SPAN = 128
CHUNKS = 3
UP = 8
DOWN_PIECE = 1
NEAR = 2
EARLY_BLOCKS = {(1, 0): (), (1, 1): (), (1, 2): (0, 1), (2, 0): (), (2, 1): (2,), (2, 2): (3,)}
TILES = ((0, 1), (), (2, 3))
PREFIX_AT = (4, 2)


def softplus(v):
    u = jnp.exp(-jnp.abs(v))
    small = u * (1.0 - u * (0.5 - u * (1.0 / 3.0 - u * 0.25)))
    return jnp.maximum(v, 0.0) + jnp.where(u < 0.02, small, jnp.log(1.0 + u))


def silu(v):
    return v / (1.0 + jnp.exp(-v))


def dot(a, b, **kw):
    return jnp.dot(a, b, preferred_element_type=jnp.float32, **kw)


def parts_of(v):
    high = v.astype(jnp.bfloat16)
    rest = v - high.astype(jnp.float32)
    middle = rest.astype(jnp.bfloat16)
    low = (rest - middle.astype(jnp.float32)).astype(jnp.bfloat16)
    return high, middle, low


def dot_t(a, b, **kw):
    return lax.dot_general(
        a, b, (((1,), (1,)), ((), ())), preferred_element_type=jnp.float32, **kw
    )


def kernel(
    n_ctx,
    decay_ref,
    skip_ref,
    step_ref,
    gain_ref,
    x_hbm,
    gate_hbm,
    maps_hbm,
    q_hbm,
    kv_hbm,
    mamba_ref,
    attn_ref,
    x_ref,
    gate_ref,
    q_ref,
    maps_raw,
    kv_raw,
    wide,
    maps_ref,
    in_sem,
    far_sem,
    kvbuf,
    qt,
    m_run,
    l_run,
    acc,
    mixed,
    decay_t,
    total_buf,
    sbuf,
    srecv,
    ebuf,
    erecv,
    sq_buf,
    up_send,
    up_recv,
    dn_send,
    dn_recv,
    sib_send,
    sib_recv,
    sibd_send,
    sibd_recv,
    y_send,
    y_recv,
    yd_send,
    yd_recv,
    d_send,
    d_recv,
    s_send,
    s_recv,
    e_send,
    e_recv,
    q_send,
    q_recv,
):
    z = lax.axis_index("ctx")
    hd = lax.axis_index("head")
    core = lax.rem(hd, 2)
    sib = hd + 1 - 2 * core
    base = hd - lax.rem(hd, 4)
    place = lax.rem(hd, 4)
    side = place // 2
    across = base + lax.rem(place + 2, 4)
    missing = core * 4 + 3 - 3 * side

    def part(c):
        return core * 4 + c + side * (3 - 2 * c)

    above = lax.rem(z + 1, n_ctx)
    below = lax.rem(z + n_ctx - 1, n_ctx)

    barrier = pltpu.get_barrier_semaphore()
    for d in range(NEAR, 0, -1):
        for other in (lax.rem(z + d, n_ctx), lax.rem(z + n_ctx - d, n_ctx)):
            pl.semaphore_signal(barrier, inc=1, device_id=(other, hd), device_id_type=MESH)
    for d in range(1, 4):
        pl.semaphore_signal(
            barrier, inc=1, device_id=(z, base + lax.rem(place + d, 4)), device_id_type=MESH
        )

    fetches = []
    for src, dst in ((kv_hbm, kv_raw), (maps_hbm, maps_raw)):
        for rows in (pl.ds(0, 4096), pl.ds(4096, 4096)):
            fetches.append((src.at[rows], dst.at[rows]))
    fetches += [(q_hbm, q_ref), (x_hbm, x_ref), (gate_hbm, gate_ref)]
    fetches = [
        pltpu.make_async_copy(src, dst, in_sem.at[i]) for i, (src, dst) in enumerate(fetches)
    ]
    for fetch in fetches:
        fetch.start()

    def pick_group(raw, waits):
        for i, fetch in enumerate(waits):
            fetch.wait()

            def widen(k, carry):
                rows = pl.ds(pl.multiple_of(i * 4096 + k * 512, 512), 512)
                wide[rows, :] = raw[rows, :].astype(jnp.float32)
                return carry

            lax.fori_loop(0, 8, widen, 0)
        return [wide[pl.ds(8 * i + hd // 4, 512, stride=16), :] for i in range(2)]

    keys, values = pick_group(kv_raw, fetches[0:2])
    for i in range(4):
        kvbuf[z, i] = keys[i * 128 : (i + 1) * 128, :].astype(jnp.bfloat16)
        kvbuf[z, 4 + i] = values[i * 128 : (i + 1) * 128, :].T.astype(jnp.bfloat16)

    def up_copy(s, c):
        block = lax.rem(z - s + n_ctx, n_ctx)
        return pltpu.make_async_remote_copy(
            src_ref=kvbuf.at[block, part(c)],
            dst_ref=kvbuf.at[block, part(c)],
            send_sem=up_send.at[s * CHUNKS + c],
            recv_sem=up_recv.at[s * CHUNKS + c],
            device_id=(above, hd),
            device_id_type=MESH,
        )

    def down_copy(s, c):
        block = lax.rem(z + s, n_ctx)
        return pltpu.make_async_remote_copy(
            src_ref=kvbuf.at[block, part(c)],
            dst_ref=kvbuf.at[block, part(c)],
            send_sem=dn_send.at[s * CHUNKS + c],
            recv_sem=dn_recv.at[s * CHUNKS + c],
            device_id=(below, hd),
            device_id_type=MESH,
        )

    def up_arrival(s, c):
        block = lax.rem(z - s + n_ctx, n_ctx)
        return pltpu.make_async_remote_copy(
            src_ref=kvbuf.at[block, part(c)],
            dst_ref=kvbuf.at[block, part(c)],
            send_sem=up_send.at[(s - 1) * CHUNKS + c],
            recv_sem=up_recv.at[(s - 1) * CHUNKS + c],
            device_id=(above, hd),
            device_id_type=MESH,
        )

    def down_arrival(s, c):
        block = lax.rem(z + s, n_ctx)
        return pltpu.make_async_remote_copy(
            src_ref=kvbuf.at[block, part(c)],
            dst_ref=kvbuf.at[block, part(c)],
            send_sem=dn_send.at[(s - 1) * CHUNKS + c],
            recv_sem=dn_recv.at[(s - 1) * CHUNKS + c],
            device_id=(below, hd),
            device_id_type=MESH,
        )

    def sib_copy(block, index, send, recv, i):
        return pltpu.make_async_remote_copy(
            src_ref=kvbuf.at[block, index],
            dst_ref=kvbuf.at[block, index],
            send_sem=send.at[i],
            recv_sem=recv.at[i],
            device_id=(z, sib),
            device_id_type=MESH,
        )

    def y_copy(block, index, send, recv, i):
        return pltpu.make_async_remote_copy(
            src_ref=kvbuf.at[block, index],
            dst_ref=kvbuf.at[block, index],
            send_sem=send.at[i],
            recv_sem=recv.at[i],
            device_id=(z, across),
            device_id_type=MESH,
        )

    def up_block(s):
        return lax.rem(z - s + n_ctx, n_ctx)

    def down_block(s):
        return lax.rem(z + s, n_ctx)

    def up_hops(c):
        return UP - 1 if c == DOWN_PIECE else UP

    def down_hops(c):
        return UP if c == DOWN_PIECE else UP - 1

    def came_up(s, c):
        return jnp.logical_and(z >= s, s <= up_hops(c))

    def travels_down(s, c):
        block = lax.rem(z + s, n_ctx)
        return jnp.logical_and(block < down_hops(c), s <= down_hops(c))

    def down_useful(s, c):
        return jnp.logical_and(z + s >= n_ctx, travels_down(s, c))

    def total_copy(d):
        return pltpu.make_async_remote_copy(
            src_ref=total_buf.at[z],
            dst_ref=total_buf.at[z],
            send_sem=d_send.at[d],
            recv_sem=d_recv.at[z],
            device_id=(lax.rem(z + d, n_ctx), hd),
            device_id_type=MESH,
        )

    def total_arrival(d):
        other = lax.rem(z + d, n_ctx)
        return pltpu.make_async_remote_copy(
            src_ref=total_buf.at[other],
            dst_ref=total_buf.at[other],
            send_sem=d_send.at[d],
            recv_sem=d_recv.at[other],
            device_id=(other, hd),
            device_id_type=MESH,
        )

    def state_copy(d):
        other = lax.rem(z + d, n_ctx)
        return pltpu.make_async_remote_copy(
            src_ref=sbuf.at[other],
            dst_ref=srecv.at[z],
            send_sem=s_send.at[d],
            recv_sem=s_recv.at[z],
            device_id=(other, hd),
            device_id_type=MESH,
        )

    def state_arrival(d):
        other = lax.rem(z + d, n_ctx)
        return pltpu.make_async_remote_copy(
            src_ref=sbuf.at[other],
            dst_ref=srecv.at[other],
            send_sem=s_send.at[d],
            recv_sem=s_recv.at[other],
            device_id=(other, hd),
            device_id_type=MESH,
        )

    def entering_copy(d):
        other = lax.rem(z + d, n_ctx)
        return pltpu.make_async_remote_copy(
            src_ref=ebuf.at[other],
            dst_ref=erecv.at[z],
            send_sem=e_send.at[d],
            recv_sem=e_recv.at[z],
            device_id=(other, hd),
            device_id_type=MESH,
        )

    def entering_arrival(d):
        other = lax.rem(z + d, n_ctx)
        return pltpu.make_async_remote_copy(
            src_ref=ebuf.at[other],
            dst_ref=erecv.at[other],
            send_sem=e_send.at[d],
            recv_sem=e_recv.at[other],
            device_id=(other, hd),
            device_id_type=MESH,
        )

    def each(first, last, action, cond=None):
        def turn(d, carry):
            if cond is None:
                action(d)
            else:

                @pl.when(cond(d))
                def _():
                    action(d)

            return carry

        lax.fori_loop(first, last, turn, 0)

    def other_of(d):
        return lax.rem(z + d, n_ctx)

    last = n_ctx - 1

    pl.semaphore_wait(barrier, 2 * NEAR + 3)
    for c in range(CHUNKS):

        @pl.when(z < n_ctx - 1)
        def _():
            up_copy(0, c).start()

        @pl.when(travels_down(0, c))
        def _():
            down_copy(0, c).start()

    def tell(i):
        d = NEAR * 2**i
        for other in (lax.rem(z + d, n_ctx), lax.rem(z + n_ctx - d, n_ctx)):
            pl.semaphore_signal(far_sem.at[i], inc=1, device_id=(other, hd), device_id_type=MESH)

    tell(0)

    step = step_ref[...]
    raw = jnp.concatenate([step[:, k * SPAN : (k + 1) * SPAN] for k in range(4)], axis=0)
    row16 = lax.broadcasted_iota(jnp.int32, (16, SPAN), 0)
    rate = jnp.zeros((16, SPAN), jnp.float32)
    for h in range(4):
        rate = jnp.where(lax.rem(row16, 4) == h, decay_ref[h], rate)
    dt = softplus(raw)
    ell = -jnp.exp(rate) * dt
    upper = (
        lax.broadcasted_iota(jnp.int32, (SPAN, SPAN), 0)
        <= lax.broadcasted_iota(jnp.int32, (SPAN, SPAN), 1)
    ).astype(jnp.float32)
    cumul = dot(ell, upper, precision=HIGH)
    ends = cumul[:, SPAN - 1 : SPAN]
    tail = jnp.exp(ends - cumul) * dt
    offsets = [jnp.zeros((4, 1), jnp.float32)]
    for k in range(4):
        offsets.append(offsets[-1] + ends[k * 4 : (k + 1) * 4])
    from_start = cumul + jnp.concatenate(offsets[:4], axis=0)
    lane2 = lax.broadcasted_iota(jnp.int32, (2, 128), 1)
    total_rows = []
    for i in range(2):
        a = jnp.broadcast_to(offsets[4][2 * i : 2 * i + 1], (1, 128))
        b = jnp.broadcast_to(offsets[4][2 * i + 1 : 2 * i + 2], (1, 128))
        total_rows.append(jnp.where(lane2[0:1] < 64, a, b))
    total_buf[z] = jnp.concatenate(total_rows, axis=0)

    b_all, c_all = pick_group(maps_raw, fetches[2:4])
    maps_ref[0] = b_all.astype(jnp.bfloat16)
    maps_ref[1] = c_all.astype(jnp.bfloat16)
    fetches[5].wait()
    row_r = lax.broadcasted_iota(jnp.int32, (16, 256), 0)
    head_l = lax.broadcasted_iota(jnp.int32, (16, 256), 1) // 64
    tail_t, start_t = (jnp.concatenate(parts_of(v.T), axis=1) for v in (tail, from_start))
    cumul_t = cumul.T
    cumul_3 = jnp.concatenate(parts_of(cumul_t), axis=1)
    running = None
    run_list = []
    for k in range(4):
        rows = slice(k * SPAN, (k + 1) * SPAN)
        pick = (row_r == k * 4 + head_l).astype(jnp.float32)
        pick_3 = jnp.concatenate([pick.astype(jnp.bfloat16)] * 3, axis=0)
        tail_x = dot(tail_t, pick_3)
        decay_t[rows, :] = jnp.exp(dot(start_t, pick_3))
        loads = (x_ref[rows, :].astype(jnp.float32) * tail_x).astype(jnp.bfloat16)
        fresh = dot(maps_ref[0, rows, :].T, loads)
        end_lane = jnp.sum(jnp.broadcast_to(ends, (16, 256)) * pick, axis=0, keepdims=True)
        running = fresh if k == 0 else jnp.exp(end_lane) * running + fresh
        run_list.append(running)
    for i in range(n_ctx):
        half, r = i // 8, i % 8
        sbuf[i] = running[r * 16 : (r + 1) * 16, half * 128 : (half + 1) * 128].astype(
            jnp.bfloat16
        )

    fetches[4].wait()
    for h in range(2):
        for i in range(4):
            qt[:, h * 512 + i * 128 : h * 512 + (i + 1) * 128] = q_ref[
                i * 128 : (i + 1) * 128, h * 128 : (h + 1) * 128
            ].T

    def send_states():
        pl.semaphore_wait(far_sem.at[1], 2)

        @pl.when(z < last)
        def _():
            each(1, n_ctx, lambda d: (total_copy(d).start(), state_copy(d).start()))

    lane_w = lax.broadcasted_iota(jnp.int32, (SPAN, SPAN), 1)
    below_diag = lax.broadcasted_iota(jnp.int32, (SPAN, SPAN), 0) >= lane_w
    lane_p = lax.broadcasted_iota(jnp.int32, (1, 256), 1) // 64
    skip = jnp.zeros((1, 256), jnp.float32)
    for h in range(4):
        skip = jnp.where(lane_p == h, skip_ref[h], skip)
    left = lane_w < 64
    def inside_block(k):
        rows = slice(k * SPAN, (k + 1) * SPAN)
        b_mat, c_mat = maps_ref[0, rows, :], maps_ref[1, rows, :]
        scores = dot_t(c_mat, b_mat)
        gate = silu(gate_ref[rows, :].astype(jnp.float32))
        decay_t[rows, :] = decay_t[rows, :] * gate
        for pair in range(2):
            lanes = slice(pair * 128, (pair + 1) * 128)
            x_pair = x_ref[rows, lanes]
            weights = []
            for h in (2 * pair, 2 * pair + 1):
                r = k * 4 + h
                spread = cumul_t[:, r : r + 1] - cumul[r : r + 1, :]
                grown = jnp.exp(jnp.where(below_diag, spread, NEG_FILL))
                weights.append((scores * grown * dt[r : r + 1, :]).astype(jnp.bfloat16))
            zero = jnp.zeros_like(x_pair)
            x_two = jnp.concatenate(
                [jnp.where(left, x_pair, zero), jnp.where(left, zero, x_pair)], axis=0
            )
            inside = dot(jnp.concatenate(weights, axis=1), x_two)
            total = inside + skip[:, lanes] * x_pair.astype(jnp.float32)
            mixed[rows, lanes] = total * gate[:, lanes]
        if k > 0:
            pick = (row_r == k * 4 + head_l).astype(jnp.bfloat16)
            grown_in = jnp.exp(dot(cumul_3, jnp.concatenate([pick] * 3, axis=0)))
            mixed[rows, :] += dot(c_mat, run_list[k - 1].astype(jnp.bfloat16)) * (grown_in * gate)

    coef = math.log2(math.e) / math.sqrt(128.0)

    def diagonal(tiles):
        def scores_of(t):
            count = (t % 4 + 1) * 128
            s = dot(kvbuf[z, 0 : t % 4 + 1].reshape(count, 128), qt[:, t * 128 : (t + 1) * 128])
            key = lax.broadcasted_iota(jnp.int32, (count, 128), 0)
            query = lax.broadcasted_iota(jnp.int32, (count, 128), 1) + t % 4 * 128
            return jnp.where(key <= query, s, NEG_FILL)

        following = scores_of(tiles[0])
        for n, t in enumerate(tiles):
            lanes = slice(t * 128, (t + 1) * 128)
            s = following
            if n + 1 < len(tiles):
                following = scores_of(tiles[n + 1])
            m = jnp.max(s, axis=0, keepdims=True)
            p = jnp.exp2((s - m) * coef)
            m_run[:, lanes] = m
            l_run[:, lanes] = jnp.sum(p, axis=0, keepdims=True)
            v_mat = jnp.concatenate([kvbuf[z, 4 + i] for i in range(t % 4 + 1)], axis=1)
            acc[:, lanes] = dot(v_mat, p.astype(jnp.bfloat16))

    ones = jnp.ones((16, 256), jnp.bfloat16)

    def attend(blocks, tiles):
        parts = [(b, i) for b in blocks for i in range(2)]
        lanes_of = [slice(t * 256, (t + 1) * 256) for t in tiles]

        def scores_of(lanes):
            queries = qt[:, lanes]
            return [dot(kvbuf[b, 2 * i : 2 * i + 2].reshape(256, 128), queries) for b, i in parts]

        following = scores_of(lanes_of[0])
        for n, lanes in enumerate(lanes_of):
            scores = following
            if n + 1 < len(lanes_of):
                following = scores_of(lanes_of[n + 1])
            before = m_run[:, lanes]
            m = before
            for s in scores:
                m = jnp.maximum(m, jnp.max(s, axis=0, keepdims=True))
            scale = jnp.exp2((before - m) * coef)
            m_run[:, lanes] = m
            summed = None
            for (b, i), s in zip(parts, scores):
                p = jnp.exp2((s - m) * coef).astype(jnp.bfloat16)
                v_mat = jnp.concatenate([kvbuf[b, 4 + 2 * i], kvbuf[b, 5 + 2 * i]], axis=1)
                part = dot(jnp.concatenate([v_mat, ones], axis=0), p)
                summed = part if summed is None else summed + part
            l_run[:, lanes] = l_run[:, lanes] * scale + summed[128:129]
            acc[:, lanes] = acc[:, lanes] * scale + summed[0:128]

    def prefix():
        each(
            1,
            n_ctx,
            lambda d: (total_arrival(d).wait_recv(), state_arrival(d).wait_recv()),
            lambda d: other_of(d) < last,
        )
        srecv[z] = sbuf[z]
        half = z // 8
        entering = jnp.zeros((16, 128), jnp.float32)
        for k in range(n_ctx):
            ebuf[k] = entering.astype(jnp.bfloat16)
            if k < last:
                entering = (
                    jnp.exp(total_buf[k, pl.ds(half, 1), :]) * entering
                    + srecv[k].astype(jnp.float32)
                )
        erecv[z] = ebuf[z]
        each(1, n_ctx, lambda d: entering_copy(d).start(), lambda d: other_of(d) > 0)

    def finish_mixed():
        @pl.when(z > 0)
        def _():
            each(1, n_ctx, lambda d: entering_arrival(d).wait_recv())
            e_mat = jnp.concatenate(
                [erecv[i * 8 : (i + 1) * 8].reshape(128, 128) for i in range(2)], axis=1
            )
            for k in range(4):
                rows = slice(k * SPAN, (k + 1) * SPAN)
                mixed[rows, :] += dot(maps_ref[1, rows, :], e_mat) * decay_t[rows, :]

        ones8 = jnp.ones((8, 256), jnp.bfloat16)
        for k in range(4):
            rows = slice(k * SPAN, (k + 1) * SPAN)
            value = mixed[rows, :]
            squares = (value * value).astype(jnp.bfloat16)
            sq_buf[place, :, rows] = dot_t(ones8, squares)
        for d in range(1, 4):
            square_copy(d).start()

    def square_copy(d):
        return pltpu.make_async_remote_copy(
            src_ref=sq_buf.at[place],
            dst_ref=sq_buf.at[place],
            send_sem=q_send.at[d],
            recv_sem=q_recv.at[place],
            device_id=(z, base + lax.rem(place + d, 4)),
            device_id_type=MESH,
        )

    def square_arrival(d):
        other = lax.rem(place + d, 4)
        return pltpu.make_async_remote_copy(
            src_ref=sq_buf.at[other],
            dst_ref=sq_buf.at[other],
            send_sem=q_send.at[d],
            recv_sem=q_recv.at[other],
            device_id=(z, base + other),
            device_id_type=MESH,
        )

    def finish_norm():
        for d in range(1, 4):
            square_arrival(d).wait_recv()
        total = sq_buf[0] + sq_buf[1] + sq_buf[2] + sq_buf[3]
        inv = lax.rsqrt(total * (1.0 / 1024.0) + EPSILON)
        i_parts = [v[0:1] for v in parts_of(inv)]
        g_parts = parts_of(gain_ref[...].reshape(1, 256))
        pairs = [(0, 0), (0, 1), (1, 0), (1, 1), (0, 2), (2, 0)]
        row16 = lax.broadcasted_iota(jnp.int32, (16, 512), 0)
        left_rows = jnp.zeros((16, 512), jnp.float32)
        right_rows = jnp.zeros((16, 256), jnp.float32)
        for r, (a, b) in enumerate(pairs):
            left_rows = jnp.where(row16 == r, i_parts[a].astype(jnp.float32), left_rows)
            right_rows = jnp.where(row16[:, :256] == r, g_parts[b].astype(jnp.float32), right_rows)
        right_rows = right_rows.astype(jnp.bfloat16)
        for k in range(4):
            rows = slice(k * SPAN, (k + 1) * SPAN)
            factor = dot(left_rows[:, rows].T.astype(jnp.bfloat16), right_rows)
            mamba_ref[rows, :] = (mixed[rows, :] * factor).astype(jnp.bfloat16)

    def ring(s, carry, early=False):
        for c in range(CHUNKS):

            @pl.when(came_up(s, c))
            def _():
                up_arrival(s, c).wait_recv()

                @pl.when(jnp.logical_and(z < last, s < up_hops(c)))
                def _():
                    up_copy(s, c).start()

            @pl.when(travels_down(s, c))
            def _():
                down_arrival(s, c).wait_recv()

                @pl.when(s < down_hops(c))
                def _():
                    down_copy(s, c).start()

            @pl.when(came_up(s, c))
            def _():
                if c == 0:
                    y_copy(up_block(s), part(c), y_send, y_recv, s).start()
                sib_copy(up_block(s), part(c), sib_send, sib_recv, s * 4 + c).start()

            @pl.when(down_useful(s, c))
            def _():
                if c == 0:
                    y_copy(down_block(s), part(c), yd_send, yd_recv, s).start()
                sib_copy(down_block(s), part(c), sibd_send, sibd_recv, s * 4 + c).start()

            if early:
                if s == 1:
                    if c == 0:
                        fetches[6].wait()
                    if c < 2:
                        diagonal(range(4 * c, 4 * c + 4))
                for k in EARLY_BLOCKS[s, c]:
                    inside_block(k)
                if s == 2 and c == 2:
                    send_states()
                if s == 2 and c == 1:
                    y_wait(1)
                continue
            if c == 0:
                sib_wait(s - 2)
            if c == 1:
                y_wait(s - 1)
            if TILES[c]:
                attend_two(s - 2, TILES[c])
            if c == PREFIX_AT[1]:
                pl.when(s == PREFIX_AT[0])(prefix)
                pl.when(s == jnp.where(z == 0, 4, 7))(finish_mixed)

        return carry

    def y_wait(s):
        @pl.when(jnp.logical_and(s >= 1, came_up(s, 0)))
        def _():
            y_copy(up_block(s), missing, y_send, y_recv, s).wait_recv()
            sib_copy(up_block(s), missing, sib_send, sib_recv, s * 4 + 3).start()

        @pl.when(jnp.logical_and(s >= 1, down_useful(s, 0)))
        def _():
            y_copy(down_block(s), missing, yd_send, yd_recv, s).wait_recv()
            sib_copy(down_block(s), missing, sibd_send, sibd_recv, s * 4 + 3).start()

    def theirs(index):
        return index + 4 - 8 * core

    def sib_wait(s):
        for c in range(4):
            index, like = (missing, 0) if c == 3 else (part(c), c)

            @pl.when(jnp.logical_and(s >= 1, came_up(s, like)))
            def _():
                sib_copy(up_block(s), theirs(index), sib_send, sib_recv, s * 4 + c).wait_recv()

            @pl.when(jnp.logical_and(s >= 1, down_useful(s, like)))
            def _():
                sib_copy(
                    down_block(s), theirs(index), sibd_send, sibd_recv, s * 4 + c
                ).wait_recv()

    def attend_two(s, c):
        up = jnp.logical_and(s >= 1, z >= s)
        down = jnp.logical_and(s >= 1, down_useful(s, 0))

        @pl.when(jnp.logical_and(up, down))
        def _():
            attend((up_block(s), down_block(s)), c)

        @pl.when(jnp.logical_and(up, jnp.logical_not(down)))
        def _():
            attend((up_block(s),), c)

    pl.semaphore_wait(far_sem.at[0], 2)
    tell(1)
    ring(1, 0, early=True)
    ring(2, 0, early=True)
    lax.fori_loop(3, UP + 1, ring, 0)
    sib_wait(UP - 1)
    attend_two(UP - 1, (0, 1))
    y_wait(UP)
    attend_two(UP - 1, (2, 3))
    finish_norm()
    sib_wait(UP)

    @pl.when(z >= UP)
    def _():
        attend((up_block(UP),), (0, 1, 2, 3))

    for h in range(2):
        for i in range(4):
            lanes = slice(h * 512 + i * 128, h * 512 + (i + 1) * 128)
            result = acc[:, lanes] * (1.0 / l_run[:, lanes])
            attn_ref[i * 128 : (i + 1) * 128, h * 128 : (h + 1) * 128] = result.T.astype(
                jnp.bfloat16
            )

    def sent(s, carry):
        for c in range(CHUNKS):

            @pl.when(jnp.logical_and(z < last, jnp.logical_and(z >= s, s < up_hops(c))))
            def _():
                up_copy(s, c).wait_send()

            @pl.when(jnp.logical_and(s < down_hops(c), travels_down(s, c)))
            def _():
                down_copy(s, c).wait_send()

        return carry

    def sent_here(s, carry):
        for c in range(4):
            index, like = (missing, 0) if c == 3 else (part(c), c)

            @pl.when(came_up(s, like))
            def _():
                sib_copy(up_block(s), index, sib_send, sib_recv, s * 4 + c).wait_send()
                if c == 0:
                    y_copy(up_block(s), index, y_send, y_recv, s).wait_send()

            @pl.when(down_useful(s, like))
            def _():
                sib_copy(down_block(s), index, sibd_send, sibd_recv, s * 4 + c).wait_send()
                if c == 0:
                    y_copy(down_block(s), index, yd_send, yd_recv, s).wait_send()

        return carry

    lax.fori_loop(0, UP, sent, 0)
    lax.fori_loop(1, UP + 1, sent_here, 0)

    @pl.when(z < last)
    def _():
        each(1, n_ctx, lambda d: (total_copy(d).wait_send(), state_copy(d).wait_send()))

    each(1, n_ctx, lambda d: entering_copy(d).wait_send(), lambda d: other_of(d) > 0)
    for d in range(1, 4):
        square_copy(d).wait_send()


def body(
    n_ctx,
    mixer_input,
    gate_input,
    step_raw,
    decay_log,
    skip_weight,
    state_maps,
    norm_gain,
    queries,
    keys_values,
):
    vmem = pl.BlockSpec(memory_space=pltpu.VMEM)
    smem = pl.BlockSpec(memory_space=pltpu.SMEM)
    hbm = pl.BlockSpec(memory_space=pltpu.HBM)
    dma = pltpu.SemaphoreType.DMA
    rows = mixer_input.shape[0]
    return pl.pallas_call(
        functools.partial(kernel, n_ctx),
        out_shape=(
            pltpu.VMEM((rows, 256), jnp.bfloat16),
            pltpu.VMEM((rows, 256), jnp.bfloat16),
        ),
        in_specs=[smem, smem, vmem, vmem] + [hbm] * 5,
        out_specs=(vmem, vmem),
        scratch_shapes=[
            pltpu.VMEM((rows, 256), jnp.bfloat16),
            pltpu.VMEM((rows, 256), jnp.bfloat16),
            pltpu.VMEM((rows, 256), jnp.bfloat16),
            pltpu.VMEM((rows * 16, 128), jnp.bfloat16),
            pltpu.VMEM((rows * 16, 128), jnp.bfloat16),
            pltpu.VMEM((rows * 16 + 16, 128), jnp.float32),
            pltpu.VMEM((2, rows, 128), jnp.bfloat16),
            dma((7,)),
            pltpu.SemaphoreType.REGULAR((2,)),
            pltpu.VMEM((n_ctx, 8, 128, 128), jnp.bfloat16),
            pltpu.VMEM((128, 1024), jnp.bfloat16),
            pltpu.VMEM((1, 1024), jnp.float32),
            pltpu.VMEM((1, 1024), jnp.float32),
            pltpu.VMEM((128, 1024), jnp.float32),
            pltpu.VMEM((512, 256), jnp.float32),
            pltpu.VMEM((512, 256), jnp.float32),
            pltpu.VMEM((n_ctx, 2, 128), jnp.float32),
            pltpu.VMEM((n_ctx, 16, 128), jnp.bfloat16),
            pltpu.VMEM((n_ctx, 16, 128), jnp.bfloat16),
            pltpu.VMEM((n_ctx, 16, 128), jnp.bfloat16),
            pltpu.VMEM((n_ctx, 16, 128), jnp.bfloat16),
            pltpu.VMEM((4, 8, 512), jnp.float32),
            dma((UP * CHUNKS,)),
            dma((UP * CHUNKS,)),
            dma((UP * CHUNKS,)),
            dma((UP * CHUNKS,)),
            dma(((UP + 1) * 4,)),
            dma(((UP + 1) * 4,)),
            dma(((UP + 1) * 4,)),
            dma(((UP + 1) * 4,)),
            dma((UP + 1,)),
            dma((UP + 1,)),
            dma((UP + 1,)),
            dma((UP + 1,)),
            dma((n_ctx,)),
            dma((n_ctx,)),
            dma((n_ctx,)),
            dma((n_ctx,)),
            dma((n_ctx,)),
            dma((n_ctx,)),
            dma((4,)),
            dma((4,)),
        ],
        compiler_params=pltpu.CompilerParams(
            collective_id=0, has_side_effects=True, vmem_limit_bytes=56 * 2**20
        ),
    )(
        decay_log,
        skip_weight,
        step_raw.T,
        norm_gain,
        mixer_input,
        gate_input,
        state_maps.reshape(rows * 16, 128),
        queries,
        keys_values.reshape(rows * 16, 128),
    )


def solution(mesh):
    in_specs = (
        P("ctx", "head"),
        P("ctx", "head"),
        P("ctx", "head"),
        P("head"),
        P("head"),
        P("ctx", None, None, None),
        P("head"),
        P("ctx", "head"),
        P("ctx", None, None, None),
    )
    return jax.shard_map(
        functools.partial(body, mesh.shape["ctx"]),
        mesh=mesh,
        in_specs=in_specs,
        out_specs=(P("ctx", "head"), P("ctx", "head")),
        check_vma=False,
    )
```
